256 devices in a mesh: sx: 8 (over x, z_lo), sy: 32 (over y, z_hi, core).
Axes of the slice: x: 4, y: 4, z: 8 (z_hi: 4, z_lo: 2; z = z_hi * 2 + z_lo), core: 2. Of those that a mesh axis runs over, the one named last changes fastest.
Arguments:
- coarse_vectors: bfloat16 [3, 64, 72, 288, 64], P(None, None, 'sx', 'sy'), may hold values from -0.032 to 0.032
- stiffness: float32 [40, 160, 64], P('sx', 'sy'), may hold values from 0.3 to 3
- vector_counts: int32 [8, 32], P('sx', 'sy'), may hold values from 32 to 64, as said below
Outputs:
- coarse_rows: float32 [8, 32, 9, 64, 64], P('sx')
The draws below stay inside these ranges and needn't reach their ends.
Inputs may be any that keep to these rules, and one draw needn't show every extreme that they name: vector_counts[r, c] vectors of subdomain (r, c) are used; some subdomain uses all 64.
All inputs are finite; a program needn't handle non-finite values.
Results may differ from the reference program's by a relative error of at most 0.0003.
Values may be sent and summed in bfloat16 or wider, within the bound.
No kernel may reach another device: no remote copies, remote signals or barrier semaphores. Data moves between devices by JAX's collectives and lax.ppermute only.
A program may use at most 192 MiB of HBM per device.

```python
import math
import jax
import jax.numpy as jnp
from jax import lax

VECTORS = 64
MARGIN = 2
CX = 5
CY = 5
NZ = 64
EXT_X = 9
EXT_Y = 9
NX = 40
NY = 160
N_SX = 8
N_SY = 32


def draw_vector_counts(key, part):
    key = jax.random.fold_in(key, 7)
    first_key, second_key = jax.random.split(key)
    counts = jax.random.randint(first_key, (N_SX * N_SY,), VECTORS // 2, VECTORS + 1, dtype=jnp.int32)
    chosen = jax.random.randint(second_key, (), 0, N_SX * N_SY, dtype=jnp.int32)
    counts = jnp.where(jnp.arange(N_SX * N_SY, dtype=jnp.int32) == chosen, VECTORS, counts)
    return counts.reshape(N_SX, N_SY)


def assemble_boxes(own_field, common_field, local_noise, scale, share, rough):
    global_field = own_field + share * common_field
    places_x = jnp.arange(N_SX * EXT_X, dtype=jnp.int32)
    rows = places_x // EXT_X * CX + places_x % EXT_X
    places_y = jnp.arange(N_SY * EXT_Y, dtype=jnp.int32)
    columns = places_y // EXT_Y * CY + places_y % EXT_Y
    boxed = jnp.take(global_field, rows, axis=2)
    boxed = jnp.take(boxed, columns, axis=3)
    values = scale * (boxed + rough * local_noise)
    return jnp.clip(values, -0.032, 0.032).astype(jnp.bfloat16)


def draw_coarse_vectors(key, part):
    key = jax.random.fold_in(key, 11)
    field_key, common_key, noise_key = jax.random.split(key, 3)
    global_shape = (3, VECTORS, NX + 2 * MARGIN, NY + 2 * MARGIN, NZ)
    common_shape = (3, 1, NX + 2 * MARGIN, NY + 2 * MARGIN, NZ)
    box_shape = (3, VECTORS, N_SX * EXT_X, N_SY * EXT_Y, NZ)
    own_field = jnp.clip(jax.random.normal(field_key, global_shape, jnp.float32), -4.0, 4.0)
    common_field = jnp.clip(jax.random.normal(common_key, common_shape, jnp.float32), -4.0, 4.0)
    local_noise = jnp.clip(jax.random.normal(noise_key, box_shape, jnp.float32), -4.0, 4.0)
    return assemble_boxes(own_field, common_field, local_noise, 0.004, 0.6, 0.3)


def levels(rng, shape, cuts, smallest, top_value):
    level, own = 1.0, jax.random.fold_in(rng, 6)
    for position, blocks in cuts:
        draws = jnp.exp(jax.random.uniform(jax.random.fold_in(own, position), (blocks,), jnp.float32, smallest / len(cuts), top_value / len(cuts)))
        level = level * jnp.repeat(draws, shape[position] // blocks).reshape([-1 if axis == position else 1 for axis in range(len(shape))])
    return level


def setup_inputs(seed: int = 0) -> dict:
    arg_keys = jax.random.split(jax.random.key(seed), 4)
    coarse_vectors = draw_coarse_vectors(jax.random.fold_in(arg_keys[3], 71), 0)
    stiffness = jnp.clip(jnp.exp(math.log(3.0) - 2.3025851 * jax.random.uniform(arg_keys[1], (NX, NY, NZ), jnp.float32) ** levels(arg_keys[1], (NX, NY, NZ), ((0, 8), (1, 32)), -0.2, 0.2)), 0.3, 3.0)
    vector_counts = draw_vector_counts(jax.random.fold_in(arg_keys[3], 71), 0)
    return {"coarse_vectors": coarse_vectors, "stiffness": stiffness, "vector_counts": vector_counts}


MASS = 0.5


def inside_line(first_cell, length, extent_all):
    places = first_cell + jnp.arange(length, dtype=jnp.int32)
    return ((places >= 0) & (places < extent_all)).astype(jnp.float32)


def edge_weights(stiff_rim, inside):
    stiff_in = stiff_rim * inside
    weight_x = 0.5 * (stiff_in[1:] + stiff_in[:-1]) * inside[1:] * inside[:-1]
    weight_y = 0.5 * (stiff_in[:, 1:] + stiff_in[:, :-1]) * inside[:, 1:] * inside[:, :-1]
    weight_z = 0.5 * (stiff_in[:, :, 1:] + stiff_in[:, :, :-1])
    return weight_x, weight_y, weight_z


def apply_component(padded_field, weights, component):
    weight_x, weight_y, weight_z = weights
    flux_x = weight_x * (padded_field[:, 1:] - padded_field[:, :-1])
    term_x = jnp.pad(flux_x, ((0, 0), (1, 0), (0, 0), (0, 0))) - jnp.pad(flux_x, ((0, 0), (0, 1), (0, 0), (0, 0)))
    flux_y = weight_y * (padded_field[:, :, 1:] - padded_field[:, :, :-1])
    term_y = jnp.pad(flux_y, ((0, 0), (0, 0), (1, 0), (0, 0))) - jnp.pad(flux_y, ((0, 0), (0, 0), (0, 1), (0, 0)))
    flux_z = weight_z * (padded_field[:, :, :, 1:] - padded_field[:, :, :, :-1])
    term_z = jnp.pad(flux_z, ((0, 0), (0, 0), (0, 0), (1, 0))) - jnp.pad(flux_z, ((0, 0), (0, 0), (0, 0), (0, 1)))
    factors = [1.0 + 2.0 * float(component == axis_number) for axis_number in range(3)]
    return MASS * padded_field + factors[0] * term_x + factors[1] * term_y + factors[2] * term_z


def frame_span(step, extent, strip_width):
    if step < 0:
        return 0, strip_width
    if step == 0:
        return 1, extent + 1
    return extent + 2 - strip_width, extent + 2


def own_span(step, extent, strip_width):
    if step < 0:
        return extent - strip_width, extent
    if step == 0:
        return 0, extent
    return 0, strip_width


def contract(applied, piece):
    return jnp.einsum("kxyz,lxyz->kl", applied, piece.astype(jnp.float32),
                      precision=lax.Precision.HIGHEST, preferred_element_type=jnp.float32)


def masked_block(coarse_vectors, vector_counts, row_index, col_index):
    valid = ((row_index >= 0) & (row_index < N_SX) & (col_index >= 0) & (col_index < N_SY)).astype(jnp.float32)
    row_clip = jnp.clip(row_index, 0, N_SX - 1).astype(jnp.int32)
    col_clip = jnp.clip(col_index, 0, N_SY - 1).astype(jnp.int32)
    zero_index = jnp.zeros((), jnp.int32)
    block = lax.dynamic_slice(coarse_vectors, (zero_index, zero_index, (row_clip * EXT_X).astype(jnp.int32),
                                               (col_clip * EXT_Y).astype(jnp.int32), zero_index),
                              (3, VECTORS, EXT_X, EXT_Y, NZ))
    keep_rows = (jnp.arange(VECTORS, dtype=jnp.int32) < vector_counts[row_clip, col_clip]).astype(jnp.float32) * valid
    in_x = inside_line(row_clip * CX - MARGIN, EXT_X, NX)
    in_y = inside_line(col_clip * CY - MARGIN, EXT_Y, NY)
    cell_mask = keep_rows[:, None, None] * in_x[None, :, None] * in_y[None, None, :]
    return block * cell_mask.astype(jnp.bfloat16)[None, :, :, :, None]


def reference(coarse_vectors, stiffness, vector_counts):
    strip_width = 2 * MARGIN + 1
    stiff_pad = jnp.pad(stiffness, ((MARGIN + 1, MARGIN + 1), (MARGIN + 1, MARGIN + 1), (0, 0)))

    def one_subdomain(index):
        row_index = (index // N_SY).astype(jnp.int32)
        col_index = (index % N_SY).astype(jnp.int32)
        zero_index = jnp.zeros((), jnp.int32)
        stiff_rim = lax.dynamic_slice(stiff_pad, ((row_index * CX).astype(jnp.int32), (col_index * CY).astype(jnp.int32), zero_index),
                                      (EXT_X + 2, EXT_Y + 2, NZ))
        inside = (inside_line(row_index * CX - MARGIN - 1, EXT_X + 2, NX)[:, None, None]
                  * inside_line(col_index * CY - MARGIN - 1, EXT_Y + 2, NY)[None, :, None])
        weights = edge_weights(stiff_rim, inside)
        own = masked_block(coarse_vectors, vector_counts, row_index, col_index)
        neighbours = {}
        for step_x in (-1, 0, 1):
            for step_y in (-1, 0, 1):
                neighbours[(step_x, step_y)] = masked_block(coarse_vectors, vector_counts, row_index + step_x, col_index + step_y)
        blocks = {offset: jnp.zeros((VECTORS, VECTORS), jnp.float32) for offset in neighbours}
        for component in range(3):
            padded_field = jnp.pad(own[component].astype(jnp.float32), ((0, 0), (1, 1), (1, 1), (0, 0)))
            applied = apply_component(padded_field, weights, component)
            for offset in neighbours:
                span_x = frame_span(offset[0], EXT_X, strip_width)
                span_y = frame_span(offset[1], EXT_Y, strip_width)
                part_x = own_span(offset[0], EXT_X, strip_width)
                part_y = own_span(offset[1], EXT_Y, strip_width)
                piece = neighbours[offset][component][:, part_x[0]:part_x[1], part_y[0]:part_y[1]]
                blocks[offset] = blocks[offset] + contract(applied[:, span_x[0]:span_x[1], span_y[0]:span_y[1]], piece)
        return jnp.stack([blocks[(step_x, step_y)] for step_x in (-1, 0, 1) for step_y in (-1, 0, 1)])

    result = lax.map(one_subdomain, jnp.arange(N_SX * N_SY, dtype=jnp.int32))
    return result.reshape(N_SX, N_SY, 9, VECTORS, VECTORS)
```

```python
import functools

import jax
import jax.numpy as jnp
from jax import lax
from jax.experimental import pallas as pl
from jax.experimental.pallas import tpu as pltpu
from jax.sharding import PartitionSpec as P

MARGIN = 2
CX = 5
CY = 5
MASS = 0.5
EXT = 9
STRIP = 5
VEC = 64
NZ = 64
L = 128
ROWS = 96
CODE_MAX = 32767.0
VMEM = 56 * 1024 * 1024

NT = (((1,), (1,)), ((), ()))


def pairs(values):
    low = lax.broadcasted_iota(jnp.int32, values[0].shape, 1) < NZ
    out = []
    for at in range(0, len(values), 2):
        first = values[at]
        if at + 1 < len(values):
            second = values[at + 1]
            top = jnp.where(low, first, pltpu.roll(second, NZ, 1))
            bottom = jnp.where(low, pltpu.roll(first, NZ, 1), second)
        else:
            top = jnp.where(low, first, 0.0)
            bottom = jnp.where(low, pltpu.roll(first, NZ, 1), 0.0)
        out.append(jnp.concatenate([top, bottom], axis=0))
    return out


def split(value):
    high = value.astype(jnp.bfloat16)
    low = (value - high.astype(jnp.float32)).astype(jnp.bfloat16)
    return high, low


def pack_kernel(meta, cv, own, strip_y, strip_x, corner):
    a = pl.program_id(0)
    count, mirrored, row, col = meta[0], meta[1], meta[2], meta[3]
    x = row * CX - MARGIN + a
    in_x = (x >= 0) & (x < meta[4])
    index01 = lax.broadcasted_iota(jnp.int32, (VEC, L), 0)
    lane = lax.broadcasted_iota(jnp.int32, (VEC // 2, L), 1)
    index2 = lax.broadcasted_iota(jnp.int32, (VEC // 2, L), 0) + jnp.where(lane < NZ, 0, VEC // 2)
    for b in range(EXT):
        place = jnp.where(mirrored == 1, EXT - 1 - b, b)
        y = col * CY - MARGIN + place
        keep = jnp.where(in_x & (y >= 0) & (y < meta[5]), count, 0)
        zero, one, two = (cv[component, 0, place] for component in range(3))
        mask01 = (index01 < keep).astype(jnp.float32).astype(jnp.bfloat16)
        mask2 = (index2 < keep).astype(jnp.float32).astype(jnp.bfloat16)
        both = jnp.concatenate([zero, one], axis=1) * mask01
        last = jnp.concatenate([two[: VEC // 2], two[VEC // 2 :]], axis=1) * mask2
        cell = jnp.concatenate([both, last], axis=0)
        span = slice(b * L, (b + 1) * L)
        own[0, :, span] = cell
        if b < STRIP:
            strip_y[0, :, span] = cell
        turned = EXT - 1 - b
        span = slice(turned * L, (turned + 1) * L)
        strip_x[0, :, span] = cell
        if turned < STRIP:
            corner[0, :, span] = cell


def pack(meta, cv):
    tail = lambda a, m: (jnp.maximum(a - (EXT - STRIP), 0), 0, 0)
    plain = lambda a, m: (a, 0, 0)
    return pl.pallas_call(
        pack_kernel,
        grid_spec=pltpu.PrefetchScalarGridSpec(
            num_scalar_prefetch=1,
            grid=(EXT,),
            in_specs=[pl.BlockSpec((3, 1, EXT, VEC, NZ), lambda a, m: (0, a, 0, 0, 0))],
            out_specs=[
                pl.BlockSpec((1, ROWS, EXT * L), plain),
                pl.BlockSpec((1, ROWS, STRIP * L), plain),
                pl.BlockSpec((1, ROWS, EXT * L), tail),
                pl.BlockSpec((1, ROWS, STRIP * L), tail),
            ],
        ),
        out_shape=[
            jax.ShapeDtypeStruct((EXT, ROWS, EXT * L), jnp.bfloat16),
            jax.ShapeDtypeStruct((EXT, ROWS, STRIP * L), jnp.bfloat16),
            jax.ShapeDtypeStruct((STRIP, ROWS, EXT * L), jnp.bfloat16),
            jax.ShapeDtypeStruct((STRIP, ROWS, STRIP * L), jnp.bfloat16),
        ],
        compiler_params=pltpu.CompilerParams(vmem_limit_bytes=VMEM),
        cost_estimate=pl.CostEstimate(flops=1000000, bytes_accessed=9000000, transcendentals=0),
        name="pack",
    )(meta, cv)


FRAME = EXT + 2


def weights_into(stiff, wx, wy, up, down):
    lane = lax.broadcasted_iota(jnp.int32, (FRAME, L), 1)
    inner = (lane % NZ) < NZ - 1
    wx[...] = jnp.zeros_like(wx)
    wy[...] = jnp.zeros_like(wy)
    for a in range(FRAME):
        here = stiff[a]
        if a > 0:
            other = stiff[a - 1]
            wx[a, :FRAME] = jnp.where((here > 0) & (other > 0), 0.5 * (here + other), 0.0)
        left, right = here[:-1], here[1:]
        wy[a, 1:FRAME] = jnp.where((left > 0) & (right > 0), 0.5 * (left + right), 0.0)
        above = jnp.where(inner, 0.5 * (here + pltpu.roll(here, L - 1, 1)), 0.0)
        up[a, :FRAME] = above
        down[a, :FRAME] = pltpu.roll(above, 1, 1)


def apply_cell(field, weights, a, b, ra, lane_low):
    wx, wy, up, down = weights
    wxa, wxb = wx[a, b : b + 1], wx[a + 1, b : b + 1]
    wya, wyb = wy[a, b : b + 1], wy[a, b + 1 : b + 2]
    upw, dnw = up[a, b : b + 1], down[a, b : b + 1]
    fx = jnp.where(lane_low, 3.0, 1.0)
    fy = jnp.where(lane_low, 1.0, 3.0)

    def at(da, db, rows):
        return field[ra + da, rows, (b + db) * L : (b + db + 1) * L]

    out = []
    for rows, (cx, cy, cz) in ((slice(0, VEC), (fx, fy, 1.0)), (slice(VEC, ROWS), (1.0, 1.0, 3.0))):
        xa, xb, ya, yb, zu, zd = wxa * cx, wxb * cx, wya * cy, wyb * cy, upw * cz, dnw * cz
        diagonal = MASS + (xa + xb) + (ya + yb) + (zu + zd)
        u = at(0, 0, rows)
        total = diagonal * u - xa * at(-1, 0, rows) - xb * at(1, 0, rows)
        total = total - ya * at(0, -1, rows) - yb * at(0, 1, rows)
        total = total - zu * pltpu.roll(u, L - 1, 1) - zd * pltpu.roll(u, 1, 1)
        out.append(total)
    return out


def own_kernel(u, stiff, applied01, applied2a, applied2b, self_block, wx, wy, up, down, field, acc):
    weights_into(stiff, wx, wy, up, down)
    zero = jnp.zeros((ROWS, L), jnp.float32)
    field[0] = jnp.zeros((ROWS, (FRAME + 1) * L), jnp.float32)
    field[1] = jnp.zeros((ROWS, (FRAME + 1) * L), jnp.float32)
    field[FRAME] = jnp.zeros((ROWS, (FRAME + 1) * L), jnp.float32)

    @pl.loop(0, EXT)
    def _(a):
        field[a + 2, :, 0:L] = zero
        field[a + 2, :, L : (EXT + 1) * L] = u[a].astype(jnp.float32)
        field[a + 2, :, (EXT + 1) * L : (FRAME + 1) * L] = jnp.zeros((ROWS, 2 * L), jnp.float32)

    lane_low = lax.broadcasted_iota(jnp.int32, (1, L), 1) < NZ
    weights = (wx, wy, up, down)

    @pl.loop(0, FRAME - 1)
    def _(a):
        thirds = []
        for b in range(1, FRAME):
            first, third = apply_cell(field, weights, a, b, a + 1, lane_low)
            high, low = split(first)
            applied01[a, :VEC, (b - 1) * L : b * L] = high
            applied01[a, VEC:, (b - 1) * L : b * L] = low
            thirds.append(third)
        for target, cells in ((applied2a, thirds[:EXT]), (applied2b, thirds[STRIP:])):
            for n, value in enumerate(pairs(cells)):
                high, low = split(value)
                target[a, :VEC, n * L : (n + 1) * L] = high
                target[a, VEC:, n * L : (n + 1) * L] = low

    acc[...] = jnp.zeros_like(acc)

    @pl.loop(0, EXT)
    def _(a):
        third = u[a, VEC:].astype(jnp.float32)
        third = pairs([third[:, b * L : (b + 1) * L] for b in range(EXT)])
        third = jnp.concatenate(third, axis=1).astype(jnp.bfloat16)
        acc[...] += lax.dot_general(
            applied01[a + 1, :, : EXT * L], u[a, :VEC], NT, preferred_element_type=jnp.float32
        ) + lax.dot_general(applied2a[a + 1], third, NT, preferred_element_type=jnp.float32)

    self_block[...] = acc[:VEC] + acc[VEC:]


def own(u, stiff):
    weight = jax.ShapeDtypeStruct((FRAME, 16, L), jnp.float32)
    return pl.pallas_call(
        own_kernel,
        out_shape=[
            jax.ShapeDtypeStruct((FRAME - 1, 2 * VEC, (FRAME - 1) * L), jnp.bfloat16),
            jax.ShapeDtypeStruct((FRAME - 1, 2 * VEC, 5 * L), jnp.bfloat16),
            jax.ShapeDtypeStruct((FRAME - 1, 2 * VEC, 3 * L), jnp.bfloat16),
            jax.ShapeDtypeStruct((VEC, VEC), jnp.float32),
            weight,
            weight,
            weight,
            weight,
        ],
        scratch_shapes=[
            pltpu.VMEM((FRAME + 1, ROWS, (FRAME + 1) * L), jnp.float32),
            pltpu.VMEM((2 * VEC, VEC), jnp.float32),
        ],
        compiler_params=pltpu.CompilerParams(vmem_limit_bytes=VMEM),
        cost_estimate=pl.CostEstimate(flops=300000000, bytes_accessed=12000000, transcendentals=0),
        name="own",
    )(u, stiff)


def lane_join(left, right):
    return jnp.concatenate([left, right], axis=1)


def thirds_of(ref, a, cells):
    third = ref[a, VEC:].astype(jnp.float32)
    third = pairs([third[:, b * L : (b + 1) * L] for b in range(cells)])
    return jnp.concatenate(third, axis=1).astype(jnp.bfloat16)


def cross_kernel(
    applied01, applied2a, applied2b, self_block, wx, wy, up, down, high_y, low_x, corner,
    mine, theirs, field, acc_y, acc_x, acc_c, acc_d, ah01, ah2,
):
    dot = functools.partial(lax.dot_general, dimension_numbers=NT, preferred_element_type=jnp.float32)
    acc_y[...] = jnp.zeros_like(acc_y)
    acc_x[...] = jnp.zeros_like(acc_x)
    acc_c[...] = jnp.zeros_like(acc_c)
    acc_d[...] = jnp.zeros_like(acc_d)
    first = FRAME - 1 - STRIP

    @pl.loop(0, EXT)
    def _(a):
        acc_y[...] += dot(applied01[a + 1, :, first * L :], high_y[a, :VEC]) + dot(
            applied2b[a + 1], thirds_of(high_y, a, STRIP)
        )

    field[...] = jnp.zeros_like(field)
    for a in range(STRIP):
        field[a + 2, :, 2 * L : (2 + STRIP) * L] = high_y[a].astype(jnp.float32)
    lane_low = lax.broadcasted_iota(jnp.int32, (1, L), 1) < NZ

    class Shifted:
        def __getitem__(self, key):
            a, rows, span = key
            return field[a, rows, span.start - 4 * L : span.stop - 4 * L]

    @pl.loop(0, STRIP)
    def _(a):
        thirds = []
        for n in range(STRIP):
            both, third = apply_cell(Shifted(), (wx, wy, up, down), a, n + 5, a + 1, lane_low)
            high, low = split(both)
            ah01[:VEC, n * L : (n + 1) * L] = high
            ah01[VEC:, n * L : (n + 1) * L] = low
            thirds.append(third)
        for n, value in enumerate(pairs(thirds)):
            high, low = split(value)
            ah2[:VEC, n * L : (n + 1) * L] = high
            ah2[VEC:, n * L : (n + 1) * L] = low
        acc_x[...] += dot(applied01[a, :, : EXT * L], low_x[a, :VEC]) + dot(
            applied2a[a], thirds_of(low_x, a, EXT)
        )
        acc_c[...] += dot(applied01[a, :, first * L :], corner[a, :VEC]) + dot(
            applied2b[a], thirds_of(corner, a, STRIP)
        )
        third = low_x[a, VEC:, (EXT - STRIP) * L :].astype(jnp.float32)
        third = pairs([third[:, n * L : (n + 1) * L] for n in range(STRIP)])
        third = jnp.concatenate(third, axis=1).astype(jnp.bfloat16)
        acc_d[...] += dot(ah01[...], low_x[a, :VEC, (EXT - STRIP) * L :]) + dot(ah2[...], third)

    own_block = self_block[...]
    block_y = acc_y[:VEC] + acc_y[VEC:]
    block_x = acc_x[:VEC] + acc_x[VEC:]
    block_c = acc_c[:VEC] + acc_c[VEC:]
    block_d = acc_d[:VEC] + acc_d[VEC:]
    nothing = jnp.zeros((VEC, VEC), jnp.float32)
    tiles = [lane_join(own_block, block_y), lane_join(block_x, block_d), lane_join(block_c, nothing)]
    turned = [lane_join(block_x.T, block_d.T), lane_join(nothing, block_c.T)]
    largest = functools.reduce(jnp.maximum, [jnp.abs(tile) for tile in tiles])
    largest = jnp.max(jnp.max(largest, axis=0, keepdims=True), axis=1, keepdims=True)
    exponent = jnp.clip(jnp.ceil(jnp.log2(largest)), -100.0, 120.0)
    scale = jnp.exp2(-exponent)

    def code(tile):
        size = jnp.minimum(jnp.sqrt(jnp.abs(tile) * scale) * CODE_MAX, CODE_MAX) + 0.5
        size = size.astype(jnp.int32)
        return jnp.where(tile < 0, -size, size).astype(jnp.int16)

    for n, tile in enumerate(tiles):
        mine[n * VEC : (n + 1) * VEC] = code(tile)
    for n, tile in enumerate(turned):
        theirs[n * VEC : (n + 1) * VEC] = code(tile)
    level = jnp.broadcast_to(exponent.astype(jnp.int32), (16, L))
    low_lanes = lax.broadcasted_iota(jnp.int32, (16, L), 1) < NZ
    mine[3 * VEC : 3 * VEC + 16] = jnp.where(low_lanes, level, 0).astype(jnp.int16)
    theirs[2 * VEC : 2 * VEC + 16] = jnp.where(low_lanes, 0, level).astype(jnp.int16)


def cross(applied, strips):
    total = pltpu.VMEM((2 * VEC, VEC), jnp.float32)
    return pl.pallas_call(
        cross_kernel,
        out_shape=[
            jax.ShapeDtypeStruct((3 * VEC + 16, L), jnp.int16),
            jax.ShapeDtypeStruct((2 * VEC + 16, L), jnp.int16),
        ],
        scratch_shapes=[
            pltpu.VMEM((STRIP + 2, ROWS, (STRIP + 2) * L), jnp.float32),
            total,
            total,
            total,
            total,
            pltpu.VMEM((2 * VEC, STRIP * L), jnp.bfloat16),
            pltpu.VMEM((2 * VEC, 3 * L), jnp.bfloat16),
        ],
        compiler_params=pltpu.CompilerParams(vmem_limit_bytes=VMEM),
        cost_estimate=pl.CostEstimate(flops=500000000, bytes_accessed=9000000, transcendentals=0),
        name="cross",
    )(*applied, *strips)


PAY = 4 * VEC + 16
GROUP = 4


def decode_kernel(meta, here, there, out):
    mirrored = meta[0] == 1
    my_y, my_z, my_core = meta[1], meta[2], meta[3]
    total = 32

    def tile(c, part, rows):
        d_y = (c // 8 - my_y) & 3
        d_z = ((c % 8) // 2 - my_z) & 3
        slot = d_y * 4 + d_z
        away = (c % 2) != my_core
        one = here[slot, part : part + rows].astype(jnp.int32)
        two = there[slot, part : part + rows].astype(jnp.int32)
        return jnp.where(away, two, one).astype(jnp.float32)

    def levels(c):
        level = tile(c, 4 * VEC, 16)
        level = jnp.exp2(level) * (1.0 / (CODE_MAX * CODE_MAX))
        return level[0:1, 0:1], level[0:1, NZ : NZ + 1]

    def value(code, scale):
        return code * jnp.abs(code) * scale

    i_y = jnp.where(mirrored, 3, 5)
    i_yt = jnp.where(mirrored, 5, 3)
    i_c = jnp.where(mirrored, 0, 2)
    i_d = jnp.where(mirrored, 2, 0)
    i_dn = jnp.where(mirrored, 8, 6)
    i_cn = jnp.where(mirrored, 6, 8)
    step = jnp.where(mirrored, 1, -1)
    for n in range(GROUP):
        c = pl.program_id(0) * GROUP + n
        from_own = (c + step + total) & (total - 1)
        from_next = (c - step + total) & (total - 1)
        mine, next_row = levels(c)
        tile0 = value(tile(c, 0, VEC), mine)
        out[0, n, 4] = tile0[:, :NZ]
        out[0, n, i_y] = tile0[:, NZ:]
        tile1 = value(tile(c, VEC, VEC), mine)
        out[0, n, 1] = tile1[:, :NZ]
        tile2 = value(tile(c, 2 * VEC, VEC), next_row)
        out[0, n, 7] = tile2[:, :NZ]
        out[0, n, i_dn] = tile2[:, NZ:]
        tile3 = value(tile(c, 3 * VEC, VEC), mine)
        out[0, n, i_c] = tile3[:, :NZ]
        mine, _ = levels(from_own)
        tile0 = value(tile(from_own, 0, VEC), mine)
        out[0, n, i_yt] = tile0[:, NZ:].T
        tile1 = value(tile(from_own, VEC, VEC), mine)
        out[0, n, i_d] = tile1[:, NZ:]
        _, next_row = levels(from_next)
        tile3 = value(tile(from_next, 3 * VEC, VEC), next_row)
        out[0, n, i_cn] = tile3[:, NZ:]


def decode(meta, here, there, columns):
    whole = pl.BlockSpec((16, PAY, L), lambda g, m: (0, 0, 0))
    return pl.pallas_call(
        decode_kernel,
        grid_spec=pltpu.PrefetchScalarGridSpec(
            num_scalar_prefetch=1,
            grid=(columns // GROUP,),
            in_specs=[whole, whole],
            out_specs=pl.BlockSpec((1, GROUP, 9, VEC, VEC), lambda g, m: (0, g, 0, 0, 0)),
        ),
        out_shape=jax.ShapeDtypeStruct((1, columns, 9, VEC, VEC), jnp.float32),
        compiler_params=pltpu.CompilerParams(vmem_limit_bytes=VMEM),
        cost_estimate=pl.CostEstimate(flops=10000000, bytes_accessed=12000000, transcendentals=0),
        name="decode",
    )(meta, here, there)


def padded_2(x, sides, width):
    for axis, dim in sides:
        peers, length = (lax.axis_size(axis), x.shape[dim])
        up = [(i, (i + 1) % peers) for i in range(peers - 1)]
        down = [(j, i) for i, j in up]
        last = lax.slice_in_dim(x, length - width, length, axis=dim)
        initial = lax.slice_in_dim(x, 0, width, axis=dim)
        before = lax.ppermute(last, axis, up)
        after = lax.ppermute(initial, axis, down)
        x = jnp.concatenate([before, x, after], axis=dim)
    return x


def body(coarse_vectors, stiffness, vector_counts):
    rows, columns = lax.axis_size("sx"), lax.axis_size("sy")
    row, col = lax.axis_index("sx"), lax.axis_index("sy")
    mirrored = 1 - row % 2
    meta = jnp.stack([vector_counts[0, 0], mirrored, row, col, jnp.int32(CX * rows), jnp.int32(CY * columns)])
    cv = jnp.transpose(coarse_vectors, (0, 2, 3, 1, 4))

    rim = padded_2(stiffness, (("sx", 0), ("sy", 1)), MARGIN + 1)
    u, strip_y, strip_x, corner = pack(meta.astype(jnp.int32), cv)

    both = ("sx", "sy")
    number = lambda r, c: r * columns + c
    side, diagonal = [], []
    for r in range(rows):
        toward = 1 if r % 2 else -1
        for c in range(columns):
            if 0 <= c + toward < columns:
                side.append((number(r, c + toward), number(r, c)))
                if r > 0:
                    diagonal.append((number(r - 1, c + toward), number(r, c)))
    return_x = [(r, r + 1) for r in range(rows - 1)]
    high_y = lax.ppermute(strip_y, both, side)
    low_x = lax.ppermute(strip_x, "sx", return_x)
    far = lax.ppermute(corner, both, diagonal)

    rim = jnp.where(mirrored == 1, rim[:, ::-1], rim)
    rim = jnp.concatenate([rim, rim], axis=2)
    applied = own(u, rim)
    mine, theirs = cross(applied, (high_y, low_x, far))
    got = lax.ppermute(theirs, "sx", [(r + 1, r) for r in range(rows - 1)])
    pay = jnp.concatenate(
        [mine[: 2 * VEC], got[:VEC], mine[2 * VEC : 3 * VEC] + got[VEC : 2 * VEC], mine[3 * VEC :] + got[2 * VEC :]],
        axis=0,
    )

    def ring(d_y, d_z, d_core):
        out = []
        for target in range(columns):
            y, z, core = target // 8, target % 8 // 2, target % 2
            out.append(((y + d_y) % 4 * 8 + (z + d_z) % 4 * 2 + (core ^ d_core), target))
        return out

    def around(x, one, other):
        half = x.shape[0] // 2
        ahead = lax.ppermute(x, "sy", one)
        behind = lax.ppermute(x, "sy", other)
        far_a = lax.ppermute(ahead[:half], "sy", one)
        far_b = lax.ppermute(behind[half:], "sy", other)
        return x, ahead, (far_a, far_b), behind

    x, ahead, (far_a, far_b), behind = around(pay, ring(0, 1, 0), ring(0, -1, 0))
    line = jnp.stack([x, ahead, jnp.concatenate([far_a, far_b], axis=0), behind])
    x, ahead, (far_a, far_b), behind = around(line, ring(1, 0, 0), ring(-1, 0, 0))
    here = jnp.concatenate([x, ahead, far_a, far_b, behind], axis=0)
    there = lax.ppermute(here, "sy", ring(0, 0, 1))
    place = jnp.stack([mirrored, col // 8, col % 8 // 2, col % 2]).astype(jnp.int32)
    return decode(place, here, there, columns)


def solution(mesh):
    return jax.shard_map(
        body,
        mesh=mesh,
        in_specs=(P(None, None, "sx", "sy", None), P("sx", "sy", None), P("sx", "sy")),
        out_specs=P("sx", None, None, None, None),
        check_vma=False,
    )
```

```python
import functools

import jax
import jax.numpy as jnp
from jax import lax
from jax.experimental import pallas as pl
from jax.experimental.pallas import tpu as pltpu
from jax.sharding import PartitionSpec as P

MARGIN = 2
CX = 5
CY = 5
MASS = 0.5
EXT = 9
STRIP = 5
ABOVE = EXT - STRIP
VEC = 64
NZ = 64
L = 128
ROWS = 96
CODE_MAX = 32767.0
MIB = 1024 * 1024
VMEM = 56 * MIB

NT = (((1,), (1,)), ((), ()))


def pairs(values):
    low = lax.broadcasted_iota(jnp.int32, values[0].shape, 1) < NZ
    out = []
    for at in range(0, len(values), 2):
        first = values[at]
        if at + 1 < len(values):
            second = values[at + 1]
            top = jnp.where(low, first, pltpu.roll(second, NZ, 1))
            bottom = jnp.where(low, pltpu.roll(first, NZ, 1), second)
        else:
            top = jnp.where(low, first, 0.0)
            bottom = jnp.where(low, pltpu.roll(first, NZ, 1), 0.0)
        out.append(jnp.concatenate([top, bottom], axis=0))
    return out


def split(value):
    high = value.astype(jnp.bfloat16)
    low = (value - high.astype(jnp.float32)).astype(jnp.bfloat16)
    return high, low


def pack_kernel(counts, cv, *refs):
    outs, stages, (rows, mask, sems, out_sems) = refs[:4], refs[4:8], refs[8:]
    own, strip, below_a, below_b = stages
    row, col = lax.axis_index("sx"), lax.axis_index("sy")
    count, mirrored = counts[0, 0], 1 - lax.rem(row, 2)
    cells_x, cells_y = CX * lax.axis_size("sx"), CY * lax.axis_size("sy")

    def fetch(a):
        return pltpu.make_async_copy(cv.at[:, a], rows.at[a], sems.at[a])

    def leave(n, a):
        return pltpu.make_async_copy(stages[n].at[a], outs[n].at[a], out_sems.at[n, a])

    @pl.loop(0, EXT)
    def _(a):
        fetch(a).start()

    index01 = lax.broadcasted_iota(jnp.int32, (VEC, L), 0)
    lane = lax.broadcasted_iota(jnp.int32, (VEC // 2, L), 1)
    index2 = lax.broadcasted_iota(jnp.int32, (VEC // 2, L), 0) + jnp.where(lane < NZ, 0, VEC // 2)
    index = jnp.concatenate([index01, index2], axis=0)
    mask[0] = jnp.zeros((ROWS, L), jnp.bfloat16)
    mask[1] = (index < count).astype(jnp.float32).astype(jnp.bfloat16)

    def cells(a):
        fetch(a).wait()
        x = row * CX - MARGIN + a
        in_x = (x >= 0) & (x < cells_x)
        for b in range(EXT):
            place = jnp.where(mirrored == 1, EXT - 1 - b, b)
            y = col * CY - MARGIN + place
            keep = jnp.where(in_x & (y >= 0) & (y < cells_y), 1, 0)
            zero, one, two = (rows[a, component, place] for component in range(3))
            both = jnp.concatenate([zero, one], axis=1)
            last = jnp.concatenate([two[: VEC // 2], two[VEC // 2 :]], axis=1)
            cell = jnp.concatenate([both, last], axis=0) * mask[keep]
            own[a, :, b * L : (b + 1) * L] = cell
            if b < STRIP:
                strip[a, :, b * L : (b + 1) * L] = cell
            yield EXT - 1 - b, cell
        leave(1, a).start()
        leave(0, a).start()

    @pl.loop(0, ABOVE)
    def _(a):
        for _ in cells(a):
            pass

    @pl.loop(ABOVE, EXT)
    def _(a):
        at = a - ABOVE
        for b, cell in cells(a):
            if b < STRIP:
                below_a[at, :, b * L : (b + 1) * L] = cell
            else:
                below_b[at, :, (b - STRIP) * L : (b - STRIP + 1) * L] = cell
        for n in (2, 3):
            leave(n, at).start()

    for n, stage in enumerate(stages):
        @pl.loop(0, stage.shape[0])
        def _(a):
            leave(n, a).wait()


def pack(meta, cv):
    shapes = [
        (EXT, ROWS, EXT * L),
        (EXT, ROWS, STRIP * L),
        (STRIP, ROWS, STRIP * L),
        (STRIP, ROWS, ABOVE * L),
    ]
    anywhere = pl.BlockSpec(memory_space=pl.ANY)
    return pl.pallas_call(
        pack_kernel,
        in_specs=[pl.BlockSpec(memory_space=pltpu.SMEM), anywhere],
        out_specs=[anywhere] * 4,
        out_shape=[jax.ShapeDtypeStruct(shape, jnp.bfloat16) for shape in shapes],
        scratch_shapes=[pltpu.VMEM(shape, jnp.bfloat16) for shape in shapes]
        + [
            pltpu.VMEM((EXT, 3, EXT, VEC, NZ), jnp.bfloat16),
            pltpu.VMEM((2, ROWS, L), jnp.bfloat16),
            pltpu.SemaphoreType.DMA((EXT,)),
            pltpu.SemaphoreType.DMA((4, EXT)),
        ],
        compiler_params=pltpu.CompilerParams(vmem_limit_bytes=VMEM),
        cost_estimate=pl.CostEstimate(flops=4000000000, bytes_accessed=9000000, transcendentals=0),
        name="pack",
    )(meta, cv)


FRAME = EXT + 2


def weights_into(stiff, wx, wy, up, down):
    lane = lax.broadcasted_iota(jnp.int32, (FRAME, L), 1)
    inner = (lane % NZ) < NZ - 1
    wx[...] = jnp.zeros_like(wx)
    wy[...] = jnp.zeros_like(wy)
    for a in range(FRAME):
        here = stiff[a]
        if a > 0:
            other = stiff[a - 1]
            wx[a, :FRAME] = jnp.where((here > 0) & (other > 0), 0.5 * (here + other), 0.0)
        left, right = here[:-1], here[1:]
        wy[a, 1:FRAME] = jnp.where((left > 0) & (right > 0), 0.5 * (left + right), 0.0)
        above = jnp.where(inner, 0.5 * (here + pltpu.roll(here, L - 1, 1)), 0.0)
        up[a, :FRAME] = above
        down[a, :FRAME] = pltpu.roll(above, 1, 1)


def apply_cell(field, weights, a, b, ra, lane_low):
    wx, wy, up, down = weights
    wxa, wxb = wx[a, b : b + 1], wx[a + 1, b : b + 1]
    wya, wyb = wy[a, b : b + 1], wy[a, b + 1 : b + 2]
    upw, dnw = up[a, b : b + 1], down[a, b : b + 1]
    fx = jnp.where(lane_low, 3.0, 1.0)
    fy = jnp.where(lane_low, 1.0, 3.0)

    def at(da, db, rows):
        return field[ra + da, rows, (b + db) * L : (b + db + 1) * L]

    out = []
    for rows, (cx, cy, cz) in ((slice(0, VEC), (fx, fy, 1.0)), (slice(VEC, ROWS), (1.0, 1.0, 3.0))):
        xa, xb, ya, yb, zu, zd = wxa * cx, wxb * cx, wya * cy, wyb * cy, upw * cz, dnw * cz
        diagonal = MASS + (xa + xb) + (ya + yb) + (zu + zd)
        u = at(0, 0, rows)
        total = diagonal * u - xa * at(-1, 0, rows) - xb * at(1, 0, rows)
        total = total - ya * at(0, -1, rows) - yb * at(0, 1, rows)
        total = total - zu * pltpu.roll(u, L - 1, 1) - zd * pltpu.roll(u, 1, 1)
        out.append(total)
    return out


FIRST = FRAME - 1 - STRIP

dot = functools.partial(lax.dot_general, dimension_numbers=NT, preferred_element_type=jnp.float32)


def total(acc):
    return acc[:VEC] + acc[VEC:]


def store_split(target, a, n, value):
    high, low = split(value)
    target[a, :VEC, n * L : (n + 1) * L] = high
    target[a, VEC:, n * L : (n + 1) * L] = low


def own_kernel(
    u, high_y, far, stiff, applied01, applied2a, applied2b, side01, side2, first_tile, first_level, far_block,
    wx, wy, up, down, field, row01, row2a, row2b, acc, acc_y, acc_c,
):
    weights_into(stiff, wx, wy, up, down)
    weights = (wx, wy, up, down)
    lane_low = lax.broadcasted_iota(jnp.int32, (1, L), 1) < NZ
    field[0] = jnp.zeros((ROWS, (FRAME + 1) * L), jnp.float32)
    field[1] = jnp.zeros((ROWS, (FRAME + 1) * L), jnp.float32)
    field[FRAME] = jnp.zeros((ROWS, (FRAME + 1) * L), jnp.float32)

    @pl.loop(0, EXT)
    def _(a):
        field[a + 2, :, 0:L] = jnp.zeros((ROWS, L), jnp.float32)
        field[a + 2, :, L : (EXT + 1) * L] = u[a].astype(jnp.float32)
        field[a + 2, :, (EXT + 1) * L : (FRAME + 1) * L] = jnp.zeros((ROWS, 2 * L), jnp.float32)

    acc[...] = jnp.zeros_like(acc)
    acc_y[...] = jnp.zeros_like(acc_y)

    def applied_row(a, to01, to2a, to2b, at):
        thirds = []
        for b in range(1, FRAME):
            first, third = apply_cell(field, weights, a, b, a + 1, lane_low)
            store_split(to01, at, b - 1, first)
            thirds.append(third)
        for target, cells in ((to2a, thirds[:EXT]), (to2b, thirds[STRIP:])):
            for n, value in enumerate(pairs(cells)):
                store_split(target, at, n, value)

    def contract_row(a, from01, from2a, from2b, at):
        acc[...] += dot(from01[at, :, : EXT * L], u[a - 1, :VEC]) + dot(from2a[at], thirds_of(u, a - 1, EXT))
        acc_y[...] += dot(from01[at, :, FIRST * L :], high_y[a - 1, :VEC]) + dot(
            from2b[at], thirds_of(high_y, a - 1, STRIP)
        )

    def contract_corner(a):
        acc_c[...] += dot(applied01[a, :, FIRST * L :], far[a, :VEC]) + dot(applied2b[a], thirds_of(far, a, STRIP))

    acc_c[...] = jnp.zeros_like(acc_c)
    applied_row(0, applied01, applied2a, applied2b, 0)
    contract_corner(0)

    @pl.loop(1, STRIP)
    def _(a):
        applied_row(a, applied01, applied2a, applied2b, a)
        contract_row(a, applied01, applied2a, applied2b, a)
        contract_corner(a)

    @pl.loop(STRIP, FRAME - 1)
    def _(a):
        applied_row(a, row01, row2a, row2b, a % 2)
        contract_row(a, row01, row2a, row2b, a % 2)

    own_block, block_y = total(acc), total(acc_y)
    level = scale_of(own_block, block_y)
    first_tile[...] = code(lane_join(own_block, block_y), level)
    first_level[...] = jnp.broadcast_to(level, (8, L))
    far_block[...] = total(acc_c)

    wide = slice(4 * L, FRAME * L)
    field[0, :, wide] = jnp.zeros((ROWS, (STRIP + 2) * L), jnp.float32)
    field[1, :, wide] = jnp.zeros((ROWS, (STRIP + 2) * L), jnp.float32)
    for a in range(STRIP):
        field[a + 2, :, 4 * L : 6 * L] = jnp.zeros((ROWS, 2 * L), jnp.float32)
        field[a + 2, :, 6 * L : FRAME * L] = high_y[a].astype(jnp.float32)

    @pl.loop(0, STRIP)
    def _(a):
        thirds = []
        for n in range(STRIP):
            both, third = apply_cell(field, weights, a, n + 5, a + 1, lane_low)
            store_split(side01, a, n, both)
            thirds.append(third)
        for n, value in enumerate(pairs(thirds)):
            store_split(side2, a, n, value)


def own(u, high_y, far, stiff):
    weight = pltpu.VMEM((FRAME, 16, L), jnp.float32)
    half = lambda width, rows=STRIP: (rows, 2 * VEC, width * L)
    acc = pltpu.VMEM((2 * VEC, VEC), jnp.float32)
    return pl.pallas_call(
        own_kernel,
        out_shape=[jax.ShapeDtypeStruct(half(width), jnp.bfloat16) for width in (FRAME - 1, 5, 3, 5, 3)]
        + coded_shapes(1)
        + [jax.ShapeDtypeStruct((VEC, VEC), jnp.float32)],
        scratch_shapes=[weight] * 4
        + [pltpu.VMEM((FRAME + 1, ROWS, (FRAME + 1) * L), jnp.float32)]
        + [pltpu.VMEM(half(width, 2), jnp.bfloat16) for width in (FRAME - 1, 5, 3)]
        + [acc, acc, acc],
        compiler_params=pltpu.CompilerParams(vmem_limit_bytes=26 * MIB),
        cost_estimate=pl.CostEstimate(flops=14000000000, bytes_accessed=30000000, transcendentals=0),
        name="own",
    )(u, high_y, far, stiff)


def coded_shapes(tiles):
    return [jax.ShapeDtypeStruct((VEC, L), jnp.int16)] * tiles + [jax.ShapeDtypeStruct((8, L), jnp.float32)]


def lane_join(left, right):
    return jnp.concatenate([left, right], axis=1)


def scale_of(*blocks):
    largest = functools.reduce(jnp.maximum, [jnp.abs(block) for block in blocks])
    largest = jnp.max(jnp.max(largest, axis=0, keepdims=True), axis=1, keepdims=True)
    return jnp.clip(jnp.ceil(jnp.log2(largest)), -100.0, 120.0)


def code(tile, exponent):
    size = jnp.minimum(jnp.sqrt(jnp.abs(tile) * jnp.exp2(-exponent)) * CODE_MAX, CODE_MAX) + 0.5
    size = size.astype(jnp.int32)
    return jnp.where(tile < 0, -size, size).astype(jnp.int16)


def thirds_of(ref, a, cells):
    third = ref[a, VEC:].astype(jnp.float32)
    third = pairs([third[:, b * L : (b + 1) * L] for b in range(cells)])
    return jnp.concatenate(third, axis=1).astype(jnp.bfloat16)


def bring(sources, slots, sems):
    def copy(n, a):
        return pltpu.make_async_copy(sources[n].at[a], slots[n].at[a], sems.at[n, a])

    def start(which=None):
        for a in range(STRIP):
            for n in range(len(sources)):
                if which is None or n in which:
                    copy(n, a).start()

    def wait(a, which=None):
        for n in range(len(sources)):
            if which is None or n in which:
                copy(n, a).wait()

    return start, wait


def row_shapes(widths):
    return [pltpu.VMEM((STRIP, rows, width * L), jnp.bfloat16) for rows, width in widths]


BELOW = ((2 * VEC, FRAME - 1), (2 * VEC, 5), (2 * VEC, 5), (2 * VEC, 3), (ROWS, STRIP), (ROWS, ABOVE))


def below_kernel(*refs):
    sources, (tile, turned, level), slots, (sems,) = refs[:6], refs[6:9], refs[9:15], refs[15:]
    start, wait = bring(sources, slots, sems)
    start()
    applied01, applied2a, side01, side2, low_a, low_b = slots
    sum_x, sum_d = [], []
    for a in range(STRIP):
        wait(a)
        thirds = [low_a[a, VEC:, b * L : (b + 1) * L].astype(jnp.float32) for b in range(STRIP)]
        thirds += [low_b[a, VEC:, b * L : (b + 1) * L].astype(jnp.float32) for b in range(ABOVE)]
        row = jnp.concatenate(pairs(thirds), axis=1).astype(jnp.bfloat16)
        sum_x += [
            dot(applied01[a, :, : STRIP * L], low_a[a, :VEC]),
            dot(applied01[a, :, STRIP * L : EXT * L], low_b[a, :VEC]),
            dot(applied2a[a], row),
        ]
        row = jnp.concatenate(pairs(thirds[ABOVE:]), axis=1).astype(jnp.bfloat16)
        sum_d += [
            dot(side01[a, :, :L], low_a[a, :VEC, ABOVE * L :]),
            dot(side01[a, :, L:], low_b[a, :VEC]),
            dot(side2[a], row),
        ]
    block_x, block_d = total(sum(sum_x)), total(sum(sum_d))
    exponent = scale_of(block_x, block_d)
    tile[...] = code(lane_join(block_x, block_d), exponent)
    turned[...] = code(lane_join(block_x.T, block_d.T), exponent)
    level[...] = jnp.broadcast_to(exponent, (8, L))


def below(applied01, applied2a, side01, side2, low_a, low_b):
    return pl.pallas_call(
        below_kernel,
        in_specs=[pl.BlockSpec(memory_space=pl.ANY)] * 6,
        out_shape=coded_shapes(2),
        scratch_shapes=row_shapes(BELOW) + [pltpu.SemaphoreType.DMA((6, STRIP))],
        compiler_params=pltpu.CompilerParams(vmem_limit_bytes=VMEM),
        cost_estimate=pl.CostEstimate(flops=2000000000, bytes_accessed=6000000, transcendentals=0),
        name="below",
    )(applied01, applied2a, side01, side2, low_a, low_b)


CORNER = ((2 * VEC, FRAME - 1), (2 * VEC, 3), (ROWS, STRIP))


def corner_kernel(meta, *refs):
    sources, coded, (mine, theirs), slots, (sems, block) = refs[:3], refs[3:9], refs[9:11], refs[11:14], refs[14:]
    far_block, first_tile, first_level, second_tile, second_turned, second_level = coded
    start, wait = bring(sources, slots, sems)
    applied01, applied2b, partner = slots

    @pl.when(meta[0] == 1)
    def _():
        start()
        parts = []
        for a in range(STRIP):
            wait(a)
            parts.append(dot(applied01[a, :, FIRST * L :], partner[a, :VEC]))
            parts.append(dot(applied2b[a], thirds_of(partner, a, STRIP)))
        block[...] = total(sum(parts))

    @pl.when(meta[0] != 1)
    def _():
        block[...] = far_block[...]

    block = block[...]
    exponent = scale_of(block)
    nothing = jnp.zeros((VEC, VEC), jnp.float32)
    mine[:VEC] = first_tile[...]
    mine[VEC : 2 * VEC] = second_tile[...]
    mine[2 * VEC : 3 * VEC] = jnp.zeros((VEC, L), jnp.int16)
    mine[3 * VEC : 4 * VEC] = code(lane_join(block, nothing), exponent)
    theirs[:VEC] = second_turned[...]
    theirs[VEC : 2 * VEC] = code(lane_join(nothing, block.T), exponent)
    row = lax.broadcasted_iota(jnp.int32, (16, L), 0)
    low = lax.broadcasted_iota(jnp.int32, (16, L), 1) < NZ
    first, second = first_level[0:1, 0:1].astype(jnp.int32), second_level[0:1, 0:1].astype(jnp.int32)
    third = exponent.astype(jnp.int32)
    own_levels = jnp.where(row == 0, first, jnp.where(row == 1, second, jnp.where((row == 3) & low, third, 0)))
    their_levels = jnp.where(row == 2, second, jnp.where((row == 3) & ~low, third, 0))
    mine[4 * VEC : 4 * VEC + 16] = own_levels.astype(jnp.int16)
    theirs[2 * VEC : 2 * VEC + 16] = their_levels.astype(jnp.int16)


def corner_and_code(meta, applied01, applied2b, partner_x, coded):
    vmem = pl.BlockSpec(memory_space=pltpu.VMEM)
    anywhere = pl.BlockSpec(memory_space=pl.ANY)
    return pl.pallas_call(
        corner_kernel,
        in_specs=[pl.BlockSpec(memory_space=pltpu.SMEM)] + [anywhere] * 3 + [vmem] * 6,
        out_shape=[
            jax.ShapeDtypeStruct((4 * VEC + 16, L), jnp.int16),
            jax.ShapeDtypeStruct((2 * VEC + 16, L), jnp.int16),
        ],
        scratch_shapes=row_shapes(CORNER)
        + [pltpu.SemaphoreType.DMA((3, STRIP)), pltpu.VMEM((VEC, VEC), jnp.float32)],
        compiler_params=pltpu.CompilerParams(vmem_limit_bytes=VMEM),
        cost_estimate=pl.CostEstimate(flops=1500000000, bytes_accessed=5000000, transcendentals=0),
        name="corner",
    )(meta, applied01, applied2b, partner_x, *coded)


def decode_kernel(meta, here, there, out, blocks, sems, columns):
    mirrored = meta[0] == 1
    my_y, my_z, my_core = meta[1], meta[2], meta[3]
    i_y = jnp.where(mirrored, 3, 5)
    i_yt = jnp.where(mirrored, 5, 3)
    i_c = jnp.where(mirrored, 0, 2)
    i_d = jnp.where(mirrored, 2, 0)
    i_dn = jnp.where(mirrored, 8, 6)
    i_cn = jnp.where(mirrored, 6, 8)
    step = jnp.where(mirrored, -1, 1)

    def spread(ref, c):
        slot = ((c // 8 - my_y) & 3) * 4 + (((c % 8) // 2 - my_z) & 3)
        to_own = (c + step + columns) & (columns - 1)
        to_next = (c - step + columns) & (columns - 1)
        level = jnp.exp2(ref[slot, 4 * VEC : 4 * VEC + 16].astype(jnp.float32)) * (1.0 / (CODE_MAX * CODE_MAX))
        def value(part):
            code = ref[slot, part * VEC : (part + 1) * VEC].astype(jnp.float32)
            return code * jnp.abs(code) * level[part : part + 1]

        tile = value(0)
        blocks[c, 4] = tile[:, :NZ]
        other = tile[:, NZ:]
        blocks[c, i_y] = other
        blocks[to_own, i_yt] = other.T
        tile = value(1)
        blocks[c, 1] = tile[:, :NZ]
        blocks[to_own, i_d] = tile[:, NZ:]
        tile = value(2)
        blocks[c, 7] = tile[:, :NZ]
        blocks[c, i_dn] = tile[:, NZ:]
        tile = value(3)
        blocks[c, i_c] = tile[:, :NZ]
        blocks[to_next, i_cn] = tile[:, NZ:]

    def both(even, odd):
        @pl.loop(0, columns // 2)
        def _(j):
            spread(even, 2 * j)
            spread(odd, 2 * j + 1)

            @pl.when(j >= 2)
            def _():
                copy(j - 1).start()

        copy(0).start()
        copy(columns // 2 - 1).start()

    def copy(j):
        return pltpu.make_async_copy(blocks.at[pl.ds(2 * j, 2)], out.at[0, pl.ds(2 * j, 2)], sems.at[j])

    @pl.when(my_core == 0)
    def _():
        both(here, there)

    @pl.when(my_core != 0)
    def _():
        both(there, here)

    @pl.loop(0, columns // 2)
    def _(j):
        copy(j).wait()


def decode(meta, here, there, columns):
    return pl.pallas_call(
        functools.partial(decode_kernel, columns=columns),
        in_specs=[pl.BlockSpec(memory_space=pltpu.SMEM)] + [pl.BlockSpec(memory_space=pltpu.VMEM)] * 2,
        out_specs=pl.BlockSpec(memory_space=pl.ANY),
        out_shape=jax.ShapeDtypeStruct((1, columns, 9, VEC, VEC), jnp.float32),
        scratch_shapes=[
            pltpu.VMEM((columns, 9, VEC, VEC), jnp.float32),
            pltpu.SemaphoreType.DMA((columns // 2,)),
        ],
        compiler_params=pltpu.CompilerParams(vmem_limit_bytes=20 * MIB),
        cost_estimate=pl.CostEstimate(flops=10000000, bytes_accessed=12000000, transcendentals=0),
        name="decode",
    )(meta, here, there)


def body(coarse_vectors, stiffness, vector_counts):
    rows, columns = lax.axis_size("sx"), lax.axis_size("sy")
    row, col = lax.axis_index("sx"), lax.axis_index("sy")
    mirrored = 1 - row % 2
    cv = jnp.transpose(coarse_vectors, (0, 2, 3, 1, 4))

    def halo(x, axis, dim):
        peers, length, width = lax.axis_size(axis), x.shape[dim], MARGIN + 1
        up = [(i, i + 1) for i in range(peers - 1)]
        down = [(j, i) for i, j in up]
        before = lax.ppermute(lax.slice_in_dim(x, length - width, length, axis=dim), axis, up)
        after = lax.ppermute(lax.slice_in_dim(x, 0, width, axis=dim), axis, down)
        return before, after

    before, after = halo(stiffness, "sx", 0)
    counts, before, after = lax.optimization_barrier((vector_counts, before, after))
    u, strip, down_a, down_b = pack(counts, cv)

    both = ("sx", "sy")
    number = lambda r, c: r * columns + c
    sides, diagonal, partner = [], [], []
    for r in range(rows):
        toward = 1 if r % 2 else -1
        for c in range(columns):
            if 0 <= c + toward < columns:
                sides.append((number(r, c + toward), number(r, c)))
                if c + toward == c ^ 1:
                    partner.append((number(r, c + toward), number(r, c)))
                elif r > 0:
                    diagonal.append((number(r - 1, c + toward), number(r, c)))
    high_y = lax.ppermute(strip, both, sides)
    far = lax.ppermute(down_a, both, diagonal)
    lines, down_a, down_b = lax.optimization_barrier(
        (jnp.concatenate([before, stiffness, after], axis=0), down_a, down_b)
    )
    before, after = halo(lines, "sy", 1)
    next_row = [(r, r + 1) for r in range(rows - 1)]
    low_a = lax.ppermute(down_a, "sx", next_row)
    low_b = lax.ppermute(down_b, "sx", next_row)

    rim = jnp.concatenate([before, lines, after], axis=1)
    rim = jnp.where(mirrored == 1, rim[:, ::-1], rim)
    rim = jnp.concatenate([rim, rim], axis=2)
    applied01, applied2a, applied2b, side01, side2, *first, far_block = own(u, high_y, far, rim)
    low_a, low_b, far_block = lax.optimization_barrier((low_a, low_b, far_block))
    partner_x = lax.ppermute(low_a, both, partner)
    second = below(applied01, applied2a, side01, side2, low_a, low_b)
    near = (col % 2 == 1 - row % 2).astype(jnp.int32)[None]
    mine, theirs = corner_and_code(near, applied01, applied2b, partner_x, (far_block, *first, *second))
    got = lax.ppermute(theirs, "sx", [(r + 1, r) for r in range(rows - 1)])
    pay = mine + jnp.pad(got, ((2 * VEC, 0), (0, 0)))

    def ring(d_y, d_z, d_core):
        out = []
        for target in range(columns):
            y, z, core = target // 8, target % 8 // 2, target % 2
            out.append(((y + d_y) % 4 * 8 + (z + d_z) % 4 * 2 + (core ^ d_core), target))
        return out

    def everyone(x, d_y, d_z):
        return [x] + [lax.ppermute(x, "sy", ring(n * d_y, n * d_z, 0)) for n in (1, 2, 3)]

    line = jnp.stack(everyone(pay, 0, 1))
    here = jnp.concatenate(everyone(line, 1, 0), axis=0)
    there = lax.ppermute(here, "sy", ring(0, 0, 1))
    place = jnp.stack([mirrored, col // 8, col % 8 // 2, col % 2]).astype(jnp.int32)
    return decode(place, here, there, columns)


def solution(mesh):
    return jax.shard_map(
        body,
        mesh=mesh,
        in_specs=(P(None, None, "sx", "sy", None), P("sx", "sy", None), P("sx", "sy")),
        out_specs=P("sx", None, None, None, None),
        check_vma=False,
    )
```

```python
import functools

import jax
import jax.numpy as jnp
from jax import lax
from jax.experimental import pallas as pl
from jax.experimental.pallas import tpu as pltpu
from jax.sharding import PartitionSpec as P

MARGIN = 2
CX = 5
CY = 5
MASS = 0.5
EXT = 9
STRIP = 5
ABOVE = EXT - STRIP
VEC = 64
NZ = 64
L = 128
ROWS = 96
CODE_MAX = 32767.0
MIB = 1024 * 1024
VMEM = 56 * MIB

NT = (((1,), (1,)), ((), ()))


def pairs(values):
    low = lax.broadcasted_iota(jnp.int32, values[0].shape, 1) < NZ
    out = []
    for at in range(0, len(values), 2):
        first = values[at]
        if at + 1 < len(values):
            second = values[at + 1]
            top = jnp.where(low, first, pltpu.roll(second, NZ, 1))
            bottom = jnp.where(low, pltpu.roll(first, NZ, 1), second)
        else:
            top = jnp.where(low, first, 0.0)
            bottom = jnp.where(low, pltpu.roll(first, NZ, 1), 0.0)
        out.append(jnp.concatenate([top, bottom], axis=0))
    return out


def split(value):
    high = value.astype(jnp.bfloat16)
    low = (value - high.astype(jnp.float32)).astype(jnp.bfloat16)
    return high, low


def pack_kernel(counts, cv, *refs):
    outs, stages, (rows, mask, sems, out_sems) = refs[:4], refs[4:8], refs[8:]
    own, strip, below_a, below_b = stages
    row, col = lax.axis_index("sx"), lax.axis_index("sy")
    count, mirrored = counts[0, 0], 1 - lax.rem(row, 2)
    cells_x, cells_y = CX * lax.axis_size("sx"), CY * lax.axis_size("sy")

    def fetch(a):
        return pltpu.make_async_copy(cv.at[:, a], rows.at[a], sems.at[a])

    def leave(n, a):
        return pltpu.make_async_copy(stages[n].at[a], outs[n].at[a], out_sems.at[n, a])

    @pl.loop(0, EXT)
    def _(a):
        fetch(a).start()

    index01 = lax.broadcasted_iota(jnp.int32, (VEC, L), 0)
    lane = lax.broadcasted_iota(jnp.int32, (VEC // 2, L), 1)
    index2 = lax.broadcasted_iota(jnp.int32, (VEC // 2, L), 0) + jnp.where(lane < NZ, 0, VEC // 2)
    index = jnp.concatenate([index01, index2], axis=0)
    mask[0] = jnp.zeros((ROWS, L), jnp.bfloat16)
    mask[1] = (index < count).astype(jnp.float32).astype(jnp.bfloat16)

    def cells(a):
        fetch(a).wait()
        x = row * CX - MARGIN + a
        in_x = (x >= 0) & (x < cells_x)
        for b in range(EXT):
            place = jnp.where(mirrored == 1, EXT - 1 - b, b)
            y = col * CY - MARGIN + place
            keep = jnp.where(in_x & (y >= 0) & (y < cells_y), 1, 0)
            zero, one, two = (rows[a, component, place] for component in range(3))
            both = jnp.concatenate([zero, one], axis=1)
            last = jnp.concatenate([two[: VEC // 2], two[VEC // 2 :]], axis=1)
            cell = jnp.concatenate([both, last], axis=0) * mask[keep]
            own[a, :, b * L : (b + 1) * L] = cell
            if b < STRIP:
                strip[a, :, b * L : (b + 1) * L] = cell
            yield EXT - 1 - b, cell
        leave(1, a).start()
        leave(0, a).start()

    @pl.loop(0, ABOVE)
    def _(a):
        for _ in cells(a):
            pass

    @pl.loop(ABOVE, EXT)
    def _(a):
        at = a - ABOVE
        for b, cell in cells(a):
            if b < STRIP:
                below_a[at, :, b * L : (b + 1) * L] = cell
            else:
                below_b[at, :, (b - STRIP) * L : (b - STRIP + 1) * L] = cell
        for n in (2, 3):
            leave(n, at).start()

    for n, stage in enumerate(stages):
        @pl.loop(0, stage.shape[0])
        def _(a):
            leave(n, a).wait()


def pack(meta, cv):
    shapes = [
        (EXT, ROWS, EXT * L),
        (EXT, ROWS, STRIP * L),
        (STRIP, ROWS, STRIP * L),
        (STRIP, ROWS, ABOVE * L),
    ]
    anywhere = pl.BlockSpec(memory_space=pl.ANY)
    return pl.pallas_call(
        pack_kernel,
        in_specs=[pl.BlockSpec(memory_space=pltpu.SMEM), anywhere],
        out_specs=[anywhere] * 4,
        out_shape=[jax.ShapeDtypeStruct(shape, jnp.bfloat16) for shape in shapes],
        scratch_shapes=[pltpu.VMEM(shape, jnp.bfloat16) for shape in shapes]
        + [
            pltpu.VMEM((EXT, 3, EXT, VEC, NZ), jnp.bfloat16),
            pltpu.VMEM((2, ROWS, L), jnp.bfloat16),
            pltpu.SemaphoreType.DMA((EXT,)),
            pltpu.SemaphoreType.DMA((4, EXT)),
        ],
        compiler_params=pltpu.CompilerParams(vmem_limit_bytes=VMEM),
        cost_estimate=pl.CostEstimate(flops=4000000000, bytes_accessed=9000000, transcendentals=0),
        name="pack",
    )(meta, cv)


FRAME = EXT + 2


def weights_into(stiff, wx, wy, up, down):
    lane = lax.broadcasted_iota(jnp.int32, (FRAME, L), 1)
    inner = (lane % NZ) < NZ - 1
    wx[...] = jnp.zeros_like(wx)
    wy[...] = jnp.zeros_like(wy)
    for a in range(FRAME):
        here = stiff[a]
        if a > 0:
            other = stiff[a - 1]
            wx[a, :FRAME] = jnp.where((here > 0) & (other > 0), 0.5 * (here + other), 0.0)
        left, right = here[:-1], here[1:]
        wy[a, 1:FRAME] = jnp.where((left > 0) & (right > 0), 0.5 * (left + right), 0.0)
        above = jnp.where(inner, 0.5 * (here + pltpu.roll(here, L - 1, 1)), 0.0)
        up[a, :FRAME] = above
        down[a, :FRAME] = pltpu.roll(above, 1, 1)


def apply_cell(field, weights, a, b, ra, lane_low):
    wx, wy, up, down = weights
    wxa, wxb = wx[a, b : b + 1], wx[a + 1, b : b + 1]
    wya, wyb = wy[a, b : b + 1], wy[a, b + 1 : b + 2]
    upw, dnw = up[a, b : b + 1], down[a, b : b + 1]
    fx = jnp.where(lane_low, 3.0, 1.0)
    fy = jnp.where(lane_low, 1.0, 3.0)

    def at(da, db, rows):
        return field[ra + da, rows, (b + db) * L : (b + db + 1) * L]

    out = []
    for rows, (cx, cy, cz) in ((slice(0, VEC), (fx, fy, 1.0)), (slice(VEC, ROWS), (1.0, 1.0, 3.0))):
        xa, xb, ya, yb, zu, zd = wxa * cx, wxb * cx, wya * cy, wyb * cy, upw * cz, dnw * cz
        diagonal = MASS + (xa + xb) + (ya + yb) + (zu + zd)
        u = at(0, 0, rows)
        total = diagonal * u - xa * at(-1, 0, rows) - xb * at(1, 0, rows)
        total = total - ya * at(0, -1, rows) - yb * at(0, 1, rows)
        total = total - zu * pltpu.roll(u, L - 1, 1) - zd * pltpu.roll(u, 1, 1)
        out.append(total)
    return out


FIRST = FRAME - 1 - STRIP

dot = functools.partial(lax.dot_general, dimension_numbers=NT, preferred_element_type=jnp.float32)


def total(acc):
    return acc[:VEC] + acc[VEC:]


def store_split(target, a, n, value):
    high, low = split(value)
    target[a, :VEC, n * L : (n + 1) * L] = high
    target[a, VEC:, n * L : (n + 1) * L] = low


def own_kernel(
    u, high_y, far, stiff, applied01, applied2a, applied2b, side01, side2, first_tile, first_level, far_block,
    wx, wy, up, down, field, row01, row2a, row2b, acc, acc_y, acc_c,
):
    weights_into(stiff, wx, wy, up, down)
    weights = (wx, wy, up, down)
    lane_low = lax.broadcasted_iota(jnp.int32, (1, L), 1) < NZ
    field[0] = jnp.zeros((ROWS, (FRAME + 1) * L), jnp.float32)
    field[1] = jnp.zeros((ROWS, (FRAME + 1) * L), jnp.float32)
    field[FRAME] = jnp.zeros((ROWS, (FRAME + 1) * L), jnp.float32)

    @pl.loop(0, EXT)
    def _(a):
        field[a + 2, :, 0:L] = jnp.zeros((ROWS, L), jnp.float32)
        field[a + 2, :, L : (EXT + 1) * L] = u[a].astype(jnp.float32)
        field[a + 2, :, (EXT + 1) * L : (FRAME + 1) * L] = jnp.zeros((ROWS, 2 * L), jnp.float32)

    acc[...] = jnp.zeros_like(acc)
    acc_y[...] = jnp.zeros_like(acc_y)

    def applied_row(a, to01, to2a, to2b, at):
        thirds = []
        for b in range(1, FRAME):
            first, third = apply_cell(field, weights, a, b, a + 1, lane_low)
            store_split(to01, at, b - 1, first)
            thirds.append(third)
        for target, cells in ((to2a, thirds[:EXT]), (to2b, thirds[STRIP:])):
            for n, value in enumerate(pairs(cells)):
                store_split(target, at, n, value)

    def contract_row(a, from01, from2a, from2b, at):
        acc[...] += dot(from01[at, :, : EXT * L], u[a - 1, :VEC]) + dot(from2a[at], thirds_of(u, a - 1, EXT))
        acc_y[...] += dot(from01[at, :, FIRST * L :], high_y[a - 1, :VEC]) + dot(
            from2b[at], thirds_of(high_y, a - 1, STRIP)
        )

    def contract_corner(a):
        acc_c[...] += dot(applied01[a, :, FIRST * L :], far[a, :VEC]) + dot(applied2b[a], thirds_of(far, a, STRIP))

    acc_c[...] = jnp.zeros_like(acc_c)
    applied_row(0, applied01, applied2a, applied2b, 0)
    contract_corner(0)

    @pl.loop(1, STRIP)
    def _(a):
        applied_row(a, applied01, applied2a, applied2b, a)
        contract_row(a, applied01, applied2a, applied2b, a)
        contract_corner(a)

    @pl.loop(STRIP, FRAME - 1)
    def _(a):
        applied_row(a, row01, row2a, row2b, a % 2)
        contract_row(a, row01, row2a, row2b, a % 2)

    own_block, block_y = total(acc), total(acc_y)
    level = scale_of(own_block, block_y)
    first_tile[...] = code(lane_join(own_block, block_y), level)
    first_level[...] = jnp.broadcast_to(level, (8, L))
    far_block[...] = total(acc_c)

    wide = slice(4 * L, FRAME * L)
    field[0, :, wide] = jnp.zeros((ROWS, (STRIP + 2) * L), jnp.float32)
    field[1, :, wide] = jnp.zeros((ROWS, (STRIP + 2) * L), jnp.float32)
    for a in range(STRIP):
        field[a + 2, :, 4 * L : 6 * L] = jnp.zeros((ROWS, 2 * L), jnp.float32)
        field[a + 2, :, 6 * L : FRAME * L] = high_y[a].astype(jnp.float32)

    @pl.loop(0, STRIP)
    def _(a):
        thirds = []
        for n in range(STRIP):
            both, third = apply_cell(field, weights, a, n + 5, a + 1, lane_low)
            store_split(side01, a, n, both)
            thirds.append(third)
        for n, value in enumerate(pairs(thirds)):
            store_split(side2, a, n, value)


def own(u, high_y, far, stiff):
    weight = pltpu.VMEM((FRAME, 16, L), jnp.float32)
    half = lambda width, rows=STRIP: (rows, 2 * VEC, width * L)
    acc = pltpu.VMEM((2 * VEC, VEC), jnp.float32)
    return pl.pallas_call(
        own_kernel,
        out_shape=[jax.ShapeDtypeStruct(half(width), jnp.bfloat16) for width in (FRAME - 1, 5, 3, 5, 3)]
        + coded_shapes(1)
        + [jax.ShapeDtypeStruct((VEC, VEC), jnp.float32)],
        scratch_shapes=[weight] * 4
        + [pltpu.VMEM((FRAME + 1, ROWS, (FRAME + 1) * L), jnp.float32)]
        + [pltpu.VMEM(half(width, 2), jnp.bfloat16) for width in (FRAME - 1, 5, 3)]
        + [acc, acc, acc],
        compiler_params=pltpu.CompilerParams(vmem_limit_bytes=26 * MIB),
        cost_estimate=pl.CostEstimate(flops=14000000000, bytes_accessed=30000000, transcendentals=0),
        name="own",
    )(u, high_y, far, stiff)


def coded_shapes(tiles):
    return [jax.ShapeDtypeStruct((VEC, L), jnp.int16)] * tiles + [jax.ShapeDtypeStruct((8, L), jnp.float32)]


def lane_join(left, right):
    return jnp.concatenate([left, right], axis=1)


def scale_of(*blocks):
    largest = functools.reduce(jnp.maximum, [jnp.abs(block) for block in blocks])
    largest = jnp.max(jnp.max(largest, axis=0, keepdims=True), axis=1, keepdims=True)
    return jnp.clip(jnp.ceil(jnp.log2(largest)), -100.0, 120.0)


def code(tile, exponent):
    size = jnp.minimum(jnp.sqrt(jnp.abs(tile) * jnp.exp2(-exponent)) * CODE_MAX, CODE_MAX) + 0.5
    size = size.astype(jnp.int32)
    return jnp.where(tile < 0, -size, size).astype(jnp.int16)


def thirds_of(ref, a, cells):
    third = ref[a, VEC:].astype(jnp.float32)
    third = pairs([third[:, b * L : (b + 1) * L] for b in range(cells)])
    return jnp.concatenate(third, axis=1).astype(jnp.bfloat16)


def bring(sources, slots, sems):
    def copy(n, a):
        return pltpu.make_async_copy(sources[n].at[a], slots[n].at[a], sems.at[n, a])

    def start(which=None):
        for a in range(STRIP):
            for n in range(len(sources)):
                if which is None or n in which:
                    copy(n, a).start()

    def wait(a, which=None):
        for n in range(len(sources)):
            if which is None or n in which:
                copy(n, a).wait()

    return start, wait


def row_shapes(widths):
    return [pltpu.VMEM((STRIP, rows, width * L), jnp.bfloat16) for rows, width in widths]


BELOW = ((2 * VEC, FRAME - 1), (2 * VEC, 5), (2 * VEC, 5), (2 * VEC, 3), (ROWS, STRIP), (ROWS, ABOVE))


def below_kernel(*refs):
    sources, (tile, turned, level), slots, (sems,) = refs[:6], refs[6:9], refs[9:15], refs[15:]
    start, wait = bring(sources, slots, sems)
    start()
    applied01, applied2a, side01, side2, low_a, low_b = slots
    sum_x, sum_d = [], []
    for a in range(STRIP):
        wait(a)
        thirds = [low_a[a, VEC:, b * L : (b + 1) * L].astype(jnp.float32) for b in range(STRIP)]
        thirds += [low_b[a, VEC:, b * L : (b + 1) * L].astype(jnp.float32) for b in range(ABOVE)]
        row = jnp.concatenate(pairs(thirds), axis=1).astype(jnp.bfloat16)
        sum_x += [
            dot(applied01[a, :, : STRIP * L], low_a[a, :VEC]),
            dot(applied01[a, :, STRIP * L : EXT * L], low_b[a, :VEC]),
            dot(applied2a[a], row),
        ]
        row = jnp.concatenate(pairs(thirds[ABOVE:]), axis=1).astype(jnp.bfloat16)
        sum_d += [
            dot(side01[a, :, :L], low_a[a, :VEC, ABOVE * L :]),
            dot(side01[a, :, L:], low_b[a, :VEC]),
            dot(side2[a], row),
        ]
    block_x, block_d = total(sum(sum_x)), total(sum(sum_d))
    exponent = scale_of(block_x, block_d)
    tile[...] = code(lane_join(block_x, block_d), exponent)
    turned[...] = code(lane_join(block_x.T, block_d.T), exponent)
    level[...] = jnp.broadcast_to(exponent, (8, L))


def below(applied01, applied2a, side01, side2, low_a, low_b):
    return pl.pallas_call(
        below_kernel,
        in_specs=[pl.BlockSpec(memory_space=pl.ANY)] * 6,
        out_shape=coded_shapes(2),
        scratch_shapes=row_shapes(BELOW) + [pltpu.SemaphoreType.DMA((6, STRIP))],
        compiler_params=pltpu.CompilerParams(vmem_limit_bytes=VMEM),
        cost_estimate=pl.CostEstimate(flops=2000000000, bytes_accessed=6000000, transcendentals=0),
        name="below",
    )(applied01, applied2a, side01, side2, low_a, low_b)


CORNER = ((2 * VEC, FRAME - 1), (2 * VEC, 3), (ROWS, STRIP))


def corner_kernel(meta, *refs):
    sources, coded, (mine, theirs), slots, (sems, block) = refs[:3], refs[3:9], refs[9:11], refs[11:14], refs[14:]
    far_block, first_tile, first_level, second_tile, second_turned, second_level = coded
    start, wait = bring(sources, slots, sems)
    applied01, applied2b, partner = slots

    @pl.when(meta[0] == 1)
    def _():
        start()
        parts = []
        for a in range(STRIP):
            wait(a)
            parts.append(dot(applied01[a, :, FIRST * L :], partner[a, :VEC]))
            parts.append(dot(applied2b[a], thirds_of(partner, a, STRIP)))
        block[...] = total(sum(parts))

    @pl.when(meta[0] != 1)
    def _():
        block[...] = far_block[...]

    block = block[...]
    exponent = scale_of(block)
    nothing = jnp.zeros((VEC, VEC), jnp.float32)
    mine[:VEC] = first_tile[...]
    mine[VEC : 2 * VEC] = second_tile[...]
    mine[2 * VEC : 3 * VEC] = jnp.zeros((VEC, L), jnp.int16)
    mine[3 * VEC : 4 * VEC] = code(lane_join(block, nothing), exponent)
    theirs[:VEC] = second_turned[...]
    theirs[VEC : 2 * VEC] = code(lane_join(nothing, block.T), exponent)
    row = lax.broadcasted_iota(jnp.int32, (16, L), 0)
    low = lax.broadcasted_iota(jnp.int32, (16, L), 1) < NZ
    first, second = first_level[0:1, 0:1].astype(jnp.int32), second_level[0:1, 0:1].astype(jnp.int32)
    third = exponent.astype(jnp.int32)
    own_levels = jnp.where(row == 0, first, jnp.where(row == 1, second, jnp.where((row == 3) & low, third, 0)))
    their_levels = jnp.where(row == 2, second, jnp.where((row == 3) & ~low, third, 0))
    mine[4 * VEC : 4 * VEC + 16] = own_levels.astype(jnp.int16)
    theirs[2 * VEC : 2 * VEC + 16] = their_levels.astype(jnp.int16)


def corner_and_code(meta, applied01, applied2b, partner_x, coded):
    vmem = pl.BlockSpec(memory_space=pltpu.VMEM)
    anywhere = pl.BlockSpec(memory_space=pl.ANY)
    return pl.pallas_call(
        corner_kernel,
        in_specs=[pl.BlockSpec(memory_space=pltpu.SMEM)] + [anywhere] * 3 + [vmem] * 6,
        out_shape=[
            jax.ShapeDtypeStruct((4 * VEC + 16, L), jnp.int16),
            jax.ShapeDtypeStruct((2 * VEC + 16, L), jnp.int16),
        ],
        scratch_shapes=row_shapes(CORNER)
        + [pltpu.SemaphoreType.DMA((3, STRIP)), pltpu.VMEM((VEC, VEC), jnp.float32)],
        compiler_params=pltpu.CompilerParams(vmem_limit_bytes=VMEM),
        cost_estimate=pl.CostEstimate(flops=1500000000, bytes_accessed=5000000, transcendentals=0),
        name="corner",
    )(meta, applied01, applied2b, partner_x, *coded)


def decode_kernel(meta, *refs, columns):
    here, there, (out, blocks, sems) = refs[:4], refs[4:8], refs[8:]
    mirrored = meta[0] == 1
    my_y, my_z, my_core = meta[1], meta[2], meta[3]
    i_y = jnp.where(mirrored, 3, 5)
    i_yt = jnp.where(mirrored, 5, 3)
    i_c = jnp.where(mirrored, 0, 2)
    i_d = jnp.where(mirrored, 2, 0)
    i_dn = jnp.where(mirrored, 8, 6)
    i_cn = jnp.where(mirrored, 6, 8)
    step = jnp.where(mirrored, -1, 1)

    def spread(ref, c, slot):
        to_own = (c + step + columns) & (columns - 1)
        to_next = (c - step + columns) & (columns - 1)
        level = jnp.exp2(ref[slot, 4 * VEC : 4 * VEC + 16].astype(jnp.float32)) * (1.0 / (CODE_MAX * CODE_MAX))

        def value(part):
            code = ref[slot, part * VEC : (part + 1) * VEC].astype(jnp.float32)
            return code * jnp.abs(code) * level[part : part + 1]

        tile = value(0)
        blocks[c, 4] = tile[:, :NZ]
        other = tile[:, NZ:]
        blocks[c, i_y] = other
        blocks[to_own, i_yt] = other.T
        tile = value(1)
        blocks[c, 1] = tile[:, :NZ]
        blocks[to_own, i_d] = tile[:, NZ:]
        tile = value(2)
        blocks[c, 7] = tile[:, :NZ]
        blocks[c, i_dn] = tile[:, NZ:]
        tile = value(3)
        blocks[c, i_c] = tile[:, :NZ]
        blocks[to_next, i_cn] = tile[:, NZ:]

    def move(first, count, sem):
        return pltpu.make_async_copy(blocks.at[pl.ds(first, count)], out.at[0, pl.ds(first, count)], sems.at[sem])

    def inner(n):
        return move(((my_y + n) & 3) * 8 + 1, 6, n)

    edges = [move(0, 1, 4), move(columns - 1, 1, 5)] + [move(8 * y - 1, 2, 5 + y) for y in (1, 2, 3)]

    def both(even, odd):
        for n in range(4):
            first = ((my_y + n) & 3) * 8

            @pl.loop(0, 2)
            def _(half):
                for z in range(2):
                    z = 2 * half + z
                    slot = (z - my_z) & 3
                    spread(even[n], first + 2 * z, slot)
                    spread(odd[n], first + 2 * z + 1, slot)

            inner(n).start()

    @pl.when(my_core == 0)
    def _():
        both(here, there)

    @pl.when(my_core != 0)
    def _():
        both(there, here)

    for copy in edges:
        copy.start()
    for copy in [inner(n) for n in range(4)] + edges:
        copy.wait()


def decode(meta, here, there, columns):
    return pl.pallas_call(
        functools.partial(decode_kernel, columns=columns),
        in_specs=[pl.BlockSpec(memory_space=pltpu.SMEM)] + [pl.BlockSpec(memory_space=pltpu.VMEM)] * 8,
        out_specs=pl.BlockSpec(memory_space=pl.ANY),
        out_shape=jax.ShapeDtypeStruct((1, columns, 9, VEC, VEC), jnp.float32),
        scratch_shapes=[pltpu.VMEM((columns, 9, VEC, VEC), jnp.float32), pltpu.SemaphoreType.DMA((9,))],
        compiler_params=pltpu.CompilerParams(vmem_limit_bytes=20 * MIB),
        cost_estimate=pl.CostEstimate(flops=10000000, bytes_accessed=12000000, transcendentals=0),
        name="decode",
    )(meta, *here, *there)


def body(coarse_vectors, stiffness, vector_counts):
    rows, columns = lax.axis_size("sx"), lax.axis_size("sy")
    row, col = lax.axis_index("sx"), lax.axis_index("sy")
    mirrored = 1 - row % 2
    cv = jnp.transpose(coarse_vectors, (0, 2, 3, 1, 4))

    def halo(x, axis, dim):
        peers, length, width = lax.axis_size(axis), x.shape[dim], MARGIN + 1
        up = [(i, i + 1) for i in range(peers - 1)]
        down = [(j, i) for i, j in up]
        before = lax.ppermute(lax.slice_in_dim(x, length - width, length, axis=dim), axis, up)
        after = lax.ppermute(lax.slice_in_dim(x, 0, width, axis=dim), axis, down)
        return before, after

    before, after = halo(stiffness, "sx", 0)
    counts, before, after = lax.optimization_barrier((vector_counts, before, after))
    u, strip, down_a, down_b = pack(counts, cv)

    both = ("sx", "sy")
    number = lambda r, c: r * columns + c
    sides, diagonal, partner = [], [], []
    for r in range(rows):
        toward = 1 if r % 2 else -1
        for c in range(columns):
            if 0 <= c + toward < columns:
                sides.append((number(r, c + toward), number(r, c)))
                if c + toward == c ^ 1:
                    partner.append((number(r, c + toward), number(r, c)))
                elif r > 0:
                    diagonal.append((number(r - 1, c + toward), number(r, c)))
    high_y = lax.ppermute(strip, both, sides)
    far = lax.ppermute(down_a, both, diagonal)
    lines, down_a, down_b = lax.optimization_barrier(
        (jnp.concatenate([before, stiffness, after], axis=0), down_a, down_b)
    )
    before, after = halo(lines, "sy", 1)
    next_row = [(r, r + 1) for r in range(rows - 1)]
    low_a = lax.ppermute(down_a, "sx", next_row)
    low_b = lax.ppermute(down_b, "sx", next_row)

    rim = jnp.concatenate([before, lines, after], axis=1)
    rim = jnp.where(mirrored == 1, rim[:, ::-1], rim)
    rim = jnp.concatenate([rim, rim], axis=2)
    applied01, applied2a, applied2b, side01, side2, *first, far_block = own(u, high_y, far, rim)
    low_a, low_b, far_block = lax.optimization_barrier((low_a, low_b, far_block))
    partner_x = lax.ppermute(low_a, both, partner)
    second = below(applied01, applied2a, side01, side2, low_a, low_b)
    near = (col % 2 == 1 - row % 2).astype(jnp.int32)[None]
    mine, theirs = corner_and_code(near, applied01, applied2b, partner_x, (far_block, *first, *second))
    got = lax.ppermute(theirs, "sx", [(r + 1, r) for r in range(rows - 1)])
    pay = mine + jnp.pad(got, ((2 * VEC, 0), (0, 0)))

    def ring(d_y, d_z, d_core):
        out = []
        for target in range(columns):
            y, z, core = target // 8, target % 8 // 2, target % 2
            out.append(((y + d_y) % 4 * 8 + (z + d_z) % 4 * 2 + (core ^ d_core), target))
        return out

    def everyone(x, d_y, d_z):
        return [x] + [lax.ppermute(x, "sy", ring(n * d_y, n * d_z, 0)) for n in (1, 2, 3)]

    line = jnp.stack(everyone(pay, 0, 1))
    here = everyone(line, 1, 0)
    there = [lax.ppermute(part, "sy", ring(0, 0, 1)) for part in here]
    place = jnp.stack([mirrored, col // 8, col % 8 // 2, col % 2]).astype(jnp.int32)
    return decode(place, here, there, columns)


def solution(mesh):
    return jax.shard_map(
        body,
        mesh=mesh,
        in_specs=(P(None, None, "sx", "sy", None), P("sx", "sy", None), P("sx", "sy")),
        out_specs=P("sx", None, None, None, None),
        check_vma=False,
    )
```

```python
import functools

import jax
import jax.numpy as jnp
from jax import lax
from jax.experimental import pallas as pl
from jax.experimental.pallas import tpu as pltpu
from jax.sharding import PartitionSpec as P

MARGIN = 2
CX = 5
CY = 5
MASS = 0.5
EXT = 9
STRIP = 5
ABOVE = EXT - STRIP
VEC = 64
NZ = 64
L = 128
ROWS = 96
CODE_MAX = 32767.0
MIB = 1024 * 1024
VMEM = 56 * MIB

NT = (((1,), (1,)), ((), ()))


def pairs(values):
    low = lax.broadcasted_iota(jnp.int32, values[0].shape, 1) < NZ
    out = []
    for at in range(0, len(values), 2):
        first = values[at]
        if at + 1 < len(values):
            second = values[at + 1]
            top = jnp.where(low, first, pltpu.roll(second, NZ, 1))
            bottom = jnp.where(low, pltpu.roll(first, NZ, 1), second)
        else:
            top = jnp.where(low, first, 0.0)
            bottom = jnp.where(low, pltpu.roll(first, NZ, 1), 0.0)
        out.append(jnp.concatenate([top, bottom], axis=0))
    return out


def split(value):
    high = value.astype(jnp.bfloat16)
    low = (value - high.astype(jnp.float32)).astype(jnp.bfloat16)
    return high, low


def pack_kernel(counts, cv, *refs):
    outs, stages, (rows, mask, sems, out_sems) = refs[:4], refs[4:8], refs[8:]
    own, strip, below_a, below_b = stages
    row, col = lax.axis_index("sx"), lax.axis_index("sy")
    count, mirrored = counts[0, 0], 1 - lax.rem(row, 2)
    cells_x, cells_y = CX * lax.axis_size("sx"), CY * lax.axis_size("sy")

    def fetch(a):
        return pltpu.make_async_copy(cv.at[:, a], rows.at[a], sems.at[a])

    def leave(n, a):
        return pltpu.make_async_copy(stages[n].at[a], outs[n].at[a], out_sems.at[n, a])

    @pl.loop(0, EXT)
    def _(a):
        fetch(a).start()

    index01 = lax.broadcasted_iota(jnp.int32, (VEC, L), 0)
    lane = lax.broadcasted_iota(jnp.int32, (VEC // 2, L), 1)
    index2 = lax.broadcasted_iota(jnp.int32, (VEC // 2, L), 0) + jnp.where(lane < NZ, 0, VEC // 2)
    index = jnp.concatenate([index01, index2], axis=0)
    mask[0] = jnp.zeros((ROWS, L), jnp.bfloat16)
    mask[1] = (index < count).astype(jnp.float32).astype(jnp.bfloat16)

    def cells(a):
        fetch(a).wait()
        x = row * CX - MARGIN + a
        in_x = (x >= 0) & (x < cells_x)
        for b in range(EXT):
            place = jnp.where(mirrored == 1, EXT - 1 - b, b)
            y = col * CY - MARGIN + place
            keep = jnp.where(in_x & (y >= 0) & (y < cells_y), 1, 0)
            zero, one, two = (rows[a, component, place] for component in range(3))
            both = jnp.concatenate([zero, one], axis=1)
            last = jnp.concatenate([two[: VEC // 2], two[VEC // 2 :]], axis=1)
            cell = jnp.concatenate([both, last], axis=0) * mask[keep]
            own[a, :, b * L : (b + 1) * L] = cell
            if b < STRIP:
                strip[a, :, b * L : (b + 1) * L] = cell
            yield EXT - 1 - b, cell
        leave(1, a).start()
        leave(0, a).start()

    @pl.loop(0, ABOVE)
    def _(a):
        for _ in cells(a):
            pass

    @pl.loop(ABOVE, EXT)
    def _(a):
        at = a - ABOVE
        for b, cell in cells(a):
            if b < STRIP:
                below_a[at, :, b * L : (b + 1) * L] = cell
            else:
                below_b[at, :, (b - STRIP) * L : (b - STRIP + 1) * L] = cell
        for n in (2, 3):
            leave(n, at).start()

    for n, stage in enumerate(stages):
        @pl.loop(0, stage.shape[0])
        def _(a):
            leave(n, a).wait()


def pack(meta, cv):
    shapes = [
        (EXT, ROWS, EXT * L),
        (EXT, ROWS, STRIP * L),
        (STRIP, ROWS, STRIP * L),
        (STRIP, ROWS, ABOVE * L),
    ]
    anywhere = pl.BlockSpec(memory_space=pl.ANY)
    return pl.pallas_call(
        pack_kernel,
        in_specs=[pl.BlockSpec(memory_space=pltpu.SMEM), anywhere],
        out_specs=[anywhere] * 4,
        out_shape=[jax.ShapeDtypeStruct(shape, jnp.bfloat16) for shape in shapes],
        scratch_shapes=[pltpu.VMEM(shape, jnp.bfloat16) for shape in shapes]
        + [
            pltpu.VMEM((EXT, 3, EXT, VEC, NZ), jnp.bfloat16),
            pltpu.VMEM((2, ROWS, L), jnp.bfloat16),
            pltpu.SemaphoreType.DMA((EXT,)),
            pltpu.SemaphoreType.DMA((4, EXT)),
        ],
        compiler_params=pltpu.CompilerParams(vmem_limit_bytes=VMEM),
        cost_estimate=pl.CostEstimate(flops=4000000000, bytes_accessed=9000000, transcendentals=0),
        name="pack",
    )(meta, cv)


FRAME = EXT + 2


def weights_into(stiff, wx, wy, up, down):
    lane = lax.broadcasted_iota(jnp.int32, (FRAME, L), 1)
    inner = (lane % NZ) < NZ - 1
    wx[...] = jnp.zeros_like(wx)
    wy[...] = jnp.zeros_like(wy)
    for a in range(FRAME):
        here = stiff[a]
        if a > 0:
            other = stiff[a - 1]
            wx[a, :FRAME] = jnp.where((here > 0) & (other > 0), 0.5 * (here + other), 0.0)
        left, right = here[:-1], here[1:]
        wy[a, 1:FRAME] = jnp.where((left > 0) & (right > 0), 0.5 * (left + right), 0.0)
        above = jnp.where(inner, 0.5 * (here + pltpu.roll(here, L - 1, 1)), 0.0)
        up[a, :FRAME] = above
        down[a, :FRAME] = pltpu.roll(above, 1, 1)


def apply_cell(field, weights, a, b, ra, lane_low):
    wx, wy, up, down = weights
    wxa, wxb = wx[a, b : b + 1], wx[a + 1, b : b + 1]
    wya, wyb = wy[a, b : b + 1], wy[a, b + 1 : b + 2]
    upw, dnw = up[a, b : b + 1], down[a, b : b + 1]
    fx = jnp.where(lane_low, 3.0, 1.0)
    fy = jnp.where(lane_low, 1.0, 3.0)

    def at(da, db, rows):
        return field[ra + da, rows, (b + db) * L : (b + db + 1) * L]

    out = []
    for rows, (cx, cy, cz) in ((slice(0, VEC), (fx, fy, 1.0)), (slice(VEC, ROWS), (1.0, 1.0, 3.0))):
        xa, xb, ya, yb, zu, zd = wxa * cx, wxb * cx, wya * cy, wyb * cy, upw * cz, dnw * cz
        diagonal = MASS + (xa + xb) + (ya + yb) + (zu + zd)
        u = at(0, 0, rows)
        total = diagonal * u - xa * at(-1, 0, rows) - xb * at(1, 0, rows)
        total = total - ya * at(0, -1, rows) - yb * at(0, 1, rows)
        total = total - zu * pltpu.roll(u, L - 1, 1) - zd * pltpu.roll(u, 1, 1)
        out.append(total)
    return out


FIRST = FRAME - 1 - STRIP

dot = functools.partial(lax.dot_general, dimension_numbers=NT, preferred_element_type=jnp.float32)


def total(acc):
    return acc[:VEC] + acc[VEC:]


def store_split(target, a, n, value):
    high, low = split(value)
    target[a, :VEC, n * L : (n + 1) * L] = high
    target[a, VEC:, n * L : (n + 1) * L] = low


def own_kernel(
    u, high_y, far, stiff, applied01, applied2a, applied2b, side01, side2, first_tile, first_level, far_block,
    wx, wy, up, down, field, row01, row2a, row2b, acc, acc_y, acc_c,
):
    weights_into(stiff, wx, wy, up, down)
    weights = (wx, wy, up, down)
    lane_low = lax.broadcasted_iota(jnp.int32, (1, L), 1) < NZ
    field[0] = jnp.zeros((ROWS, (FRAME + 1) * L), jnp.float32)
    field[1] = jnp.zeros((ROWS, (FRAME + 1) * L), jnp.float32)
    field[FRAME] = jnp.zeros((ROWS, (FRAME + 1) * L), jnp.float32)

    @pl.loop(0, EXT)
    def _(a):
        field[a + 2, :, 0:L] = jnp.zeros((ROWS, L), jnp.float32)
        field[a + 2, :, L : (EXT + 1) * L] = u[a].astype(jnp.float32)
        field[a + 2, :, (EXT + 1) * L : (FRAME + 1) * L] = jnp.zeros((ROWS, 2 * L), jnp.float32)

    acc[...] = jnp.zeros_like(acc)
    acc_y[...] = jnp.zeros_like(acc_y)

    def applied_row(a, to01, to2a, to2b, at):
        thirds = []
        for b in range(1, FRAME):
            first, third = apply_cell(field, weights, a, b, a + 1, lane_low)
            store_split(to01, at, b - 1, first)
            thirds.append(third)
        for target, cells in ((to2a, thirds[:EXT]), (to2b, thirds[STRIP:])):
            for n, value in enumerate(pairs(cells)):
                store_split(target, at, n, value)

    def contract_row(a, from01, from2a, from2b, at):
        acc[...] += dot(from01[at, :, : EXT * L], u[a - 1, :VEC]) + dot(from2a[at], thirds_of(u, a - 1, EXT))
        acc_y[...] += dot(from01[at, :, FIRST * L :], high_y[a - 1, :VEC]) + dot(
            from2b[at], thirds_of(high_y, a - 1, STRIP)
        )

    def contract_corner(a):
        acc_c[...] += dot(applied01[a, :, FIRST * L :], far[a, :VEC]) + dot(applied2b[a], thirds_of(far, a, STRIP))

    acc_c[...] = jnp.zeros_like(acc_c)
    applied_row(0, applied01, applied2a, applied2b, 0)
    contract_corner(0)

    @pl.loop(1, STRIP)
    def _(a):
        applied_row(a, applied01, applied2a, applied2b, a)
        contract_row(a, applied01, applied2a, applied2b, a)
        contract_corner(a)

    @pl.loop(STRIP, FRAME - 1)
    def _(a):
        applied_row(a, row01, row2a, row2b, a % 2)
        contract_row(a, row01, row2a, row2b, a % 2)

    own_block, block_y = total(acc), total(acc_y)
    level = scale_of(own_block, block_y)
    first_tile[...] = code(lane_join(own_block, block_y), level)
    first_level[...] = jnp.broadcast_to(level, (8, L))
    far_block[...] = total(acc_c)

    wide = slice(4 * L, FRAME * L)
    field[0, :, wide] = jnp.zeros((ROWS, (STRIP + 2) * L), jnp.float32)
    field[1, :, wide] = jnp.zeros((ROWS, (STRIP + 2) * L), jnp.float32)
    for a in range(STRIP):
        field[a + 2, :, 4 * L : 6 * L] = jnp.zeros((ROWS, 2 * L), jnp.float32)
        field[a + 2, :, 6 * L : FRAME * L] = high_y[a].astype(jnp.float32)

    @pl.loop(0, STRIP)
    def _(a):
        thirds = []
        for n in range(STRIP):
            both, third = apply_cell(field, weights, a, n + 5, a + 1, lane_low)
            store_split(side01, a, n, both)
            thirds.append(third)
        for n, value in enumerate(pairs(thirds)):
            store_split(side2, a, n, value)


def own(u, high_y, far, stiff):
    weight = pltpu.VMEM((FRAME, 16, L), jnp.float32)
    half = lambda width, rows=STRIP: (rows, 2 * VEC, width * L)
    acc = pltpu.VMEM((2 * VEC, VEC), jnp.float32)
    return pl.pallas_call(
        own_kernel,
        out_shape=[jax.ShapeDtypeStruct(half(width), jnp.bfloat16) for width in (FRAME - 1, 5, 3, 5, 3)]
        + coded_shapes(1)
        + [jax.ShapeDtypeStruct((VEC, VEC), jnp.float32)],
        scratch_shapes=[weight] * 4
        + [pltpu.VMEM((FRAME + 1, ROWS, (FRAME + 1) * L), jnp.float32)]
        + [pltpu.VMEM(half(width, 2), jnp.bfloat16) for width in (FRAME - 1, 5, 3)]
        + [acc, acc, acc],
        compiler_params=pltpu.CompilerParams(vmem_limit_bytes=VMEM),
        cost_estimate=pl.CostEstimate(flops=14000000000, bytes_accessed=30000000, transcendentals=0),
        name="own",
    )(u, high_y, far, stiff)


def coded_shapes(tiles):
    return [jax.ShapeDtypeStruct((VEC, L), jnp.int16)] * tiles + [jax.ShapeDtypeStruct((8, L), jnp.float32)]


def lane_join(left, right):
    return jnp.concatenate([left, right], axis=1)


def scale_of(*blocks):
    largest = functools.reduce(jnp.maximum, [jnp.abs(block) for block in blocks])
    largest = jnp.max(jnp.max(largest, axis=0, keepdims=True), axis=1, keepdims=True)
    return jnp.clip(jnp.ceil(jnp.log2(largest)), -100.0, 120.0)


def code(tile, exponent):
    size = jnp.minimum(jnp.sqrt(jnp.abs(tile) * jnp.exp2(-exponent)) * CODE_MAX, CODE_MAX) + 0.5
    size = size.astype(jnp.int32)
    return jnp.where(tile < 0, -size, size).astype(jnp.int16)


def thirds_of(ref, a, cells):
    third = ref[a, VEC:].astype(jnp.float32)
    third = pairs([third[:, b * L : (b + 1) * L] for b in range(cells)])
    return jnp.concatenate(third, axis=1).astype(jnp.bfloat16)


def bring(sources, slots, sems):
    def copy(n, a):
        return pltpu.make_async_copy(sources[n].at[a], slots[n].at[a], sems.at[n, a])

    def start(which=None):
        for a in range(STRIP):
            for n in range(len(sources)):
                if which is None or n in which:
                    copy(n, a).start()

    def wait(a, which=None):
        for n in range(len(sources)):
            if which is None or n in which:
                copy(n, a).wait()

    return start, wait


def row_shapes(widths):
    return [pltpu.VMEM((STRIP, rows, width * L), jnp.bfloat16) for rows, width in widths]


BELOW = ((2 * VEC, FRAME - 1), (2 * VEC, 5), (2 * VEC, 5), (2 * VEC, 3), (ROWS, STRIP), (ROWS, ABOVE))


def below_kernel(*refs):
    sources, (tile, turned, level), slots, (sems,) = refs[:6], refs[6:9], refs[9:15], refs[15:]
    start, wait = bring(sources, slots, sems)
    start()
    applied01, applied2a, side01, side2, low_a, low_b = slots
    sum_x, sum_d = [], []
    for a in range(STRIP):
        wait(a)
        thirds = [low_a[a, VEC:, b * L : (b + 1) * L].astype(jnp.float32) for b in range(STRIP)]
        thirds += [low_b[a, VEC:, b * L : (b + 1) * L].astype(jnp.float32) for b in range(ABOVE)]
        row = jnp.concatenate(pairs(thirds), axis=1).astype(jnp.bfloat16)
        sum_x += [
            dot(applied01[a, :, : STRIP * L], low_a[a, :VEC]),
            dot(applied01[a, :, STRIP * L : EXT * L], low_b[a, :VEC]),
            dot(applied2a[a], row),
        ]
        row = jnp.concatenate(pairs(thirds[ABOVE:]), axis=1).astype(jnp.bfloat16)
        sum_d += [
            dot(side01[a, :, :L], low_a[a, :VEC, ABOVE * L :]),
            dot(side01[a, :, L:], low_b[a, :VEC]),
            dot(side2[a], row),
        ]
    block_x, block_d = total(sum(sum_x)), total(sum(sum_d))
    exponent = scale_of(block_x, block_d)
    tile[...] = code(lane_join(block_x, block_d), exponent)
    turned[...] = code(lane_join(block_x.T, block_d.T), exponent)
    level[...] = jnp.broadcast_to(exponent, (8, L))


def below(applied01, applied2a, side01, side2, low_a, low_b):
    return pl.pallas_call(
        below_kernel,
        in_specs=[pl.BlockSpec(memory_space=pl.ANY)] * 6,
        out_shape=coded_shapes(2),
        scratch_shapes=row_shapes(BELOW) + [pltpu.SemaphoreType.DMA((6, STRIP))],
        compiler_params=pltpu.CompilerParams(vmem_limit_bytes=VMEM),
        cost_estimate=pl.CostEstimate(flops=2000000000, bytes_accessed=6000000, transcendentals=0),
        name="below",
    )(applied01, applied2a, side01, side2, low_a, low_b)


CORNER = ((2 * VEC, FRAME - 1), (2 * VEC, 3), (ROWS, STRIP))


def corner_kernel(meta, *refs):
    sources, coded, (mine, theirs), slots, (sems, block) = refs[:3], refs[3:9], refs[9:11], refs[11:14], refs[14:]
    far_block, first_tile, first_level, second_tile, second_turned, second_level = coded
    start, wait = bring(sources, slots, sems)
    applied01, applied2b, partner = slots

    @pl.when(meta[0] == 1)
    def _():
        start()
        parts = []
        for a in range(STRIP):
            wait(a)
            parts.append(dot(applied01[a, :, FIRST * L :], partner[a, :VEC]))
            parts.append(dot(applied2b[a], thirds_of(partner, a, STRIP)))
        block[...] = total(sum(parts))

    @pl.when(meta[0] != 1)
    def _():
        block[...] = far_block[...]

    block = block[...]
    exponent = scale_of(block)
    nothing = jnp.zeros((VEC, VEC), jnp.float32)
    mine[:VEC] = first_tile[...]
    mine[VEC : 2 * VEC] = second_tile[...]
    mine[2 * VEC : 3 * VEC] = jnp.zeros((VEC, L), jnp.int16)
    mine[3 * VEC : 4 * VEC] = code(lane_join(block, nothing), exponent)
    theirs[:VEC] = second_turned[...]
    theirs[VEC : 2 * VEC] = code(lane_join(nothing, block.T), exponent)
    row = lax.broadcasted_iota(jnp.int32, (16, L), 0)
    low = lax.broadcasted_iota(jnp.int32, (16, L), 1) < NZ
    first, second = first_level[0:1, 0:1].astype(jnp.int32), second_level[0:1, 0:1].astype(jnp.int32)
    third = exponent.astype(jnp.int32)
    own_levels = jnp.where(row == 0, first, jnp.where(row == 1, second, jnp.where((row == 3) & low, third, 0)))
    their_levels = jnp.where(row == 2, second, jnp.where((row == 3) & ~low, third, 0))
    mine[4 * VEC : 4 * VEC + 16] = own_levels.astype(jnp.int16)
    theirs[2 * VEC : 2 * VEC + 16] = their_levels.astype(jnp.int16)


def corner_and_code(meta, applied01, applied2b, partner_x, coded):
    vmem = pl.BlockSpec(memory_space=pltpu.VMEM)
    anywhere = pl.BlockSpec(memory_space=pl.ANY)
    return pl.pallas_call(
        corner_kernel,
        in_specs=[pl.BlockSpec(memory_space=pltpu.SMEM)] + [anywhere] * 3 + [vmem] * 6,
        out_shape=[
            jax.ShapeDtypeStruct((4 * VEC + 16, L), jnp.int16),
            jax.ShapeDtypeStruct((2 * VEC + 16, L), jnp.int16),
        ],
        scratch_shapes=row_shapes(CORNER)
        + [pltpu.SemaphoreType.DMA((3, STRIP)), pltpu.VMEM((VEC, VEC), jnp.float32)],
        compiler_params=pltpu.CompilerParams(vmem_limit_bytes=VMEM),
        cost_estimate=pl.CostEstimate(flops=1500000000, bytes_accessed=5000000, transcendentals=0),
        name="corner",
    )(meta, applied01, applied2b, partner_x, *coded)


def decode_kernel(meta, *refs, columns):
    here, there, (out, blocks, sems) = refs[:4], refs[4:8], refs[8:]
    mirrored = meta[0] == 1
    my_y, my_z, my_core = meta[1], meta[2], meta[3]
    i_y = jnp.where(mirrored, 3, 5)
    i_yt = jnp.where(mirrored, 5, 3)
    i_c = jnp.where(mirrored, 0, 2)
    i_d = jnp.where(mirrored, 2, 0)
    i_dn = jnp.where(mirrored, 8, 6)
    i_cn = jnp.where(mirrored, 6, 8)
    step = jnp.where(mirrored, -1, 1)

    def spread(ref, c, slot):
        to_own = (c + step + columns) & (columns - 1)
        to_next = (c - step + columns) & (columns - 1)
        level = jnp.exp2(ref[slot, 4 * VEC : 4 * VEC + 16].astype(jnp.float32)) * (1.0 / (CODE_MAX * CODE_MAX))

        def value(part):
            code = ref[slot, part * VEC : (part + 1) * VEC].astype(jnp.float32)
            return code * jnp.abs(code) * level[part : part + 1]

        tile = value(0)
        blocks[c, 4] = tile[:, :NZ]
        other = tile[:, NZ:]
        blocks[c, i_y] = other
        blocks[to_own, i_yt] = other.T
        tile = value(1)
        blocks[c, 1] = tile[:, :NZ]
        blocks[to_own, i_d] = tile[:, NZ:]
        tile = value(2)
        blocks[c, 7] = tile[:, :NZ]
        blocks[c, i_dn] = tile[:, NZ:]
        tile = value(3)
        blocks[c, i_c] = tile[:, :NZ]
        blocks[to_next, i_cn] = tile[:, NZ:]

    def move(first, count, sem):
        return pltpu.make_async_copy(blocks.at[pl.ds(first, count)], out.at[0, pl.ds(first, count)], sems.at[sem])

    def inner(n):
        return move(((my_y + n) & 3) * 8 + 1, 6, n)

    edges = [move(0, 1, 4), move(columns - 1, 1, 5)] + [move(8 * y - 1, 2, 5 + y) for y in (1, 2, 3)]

    def both(even, odd):
        for n in range(4):
            first = ((my_y + n) & 3) * 8

            @pl.loop(0, 2)
            def _(half):
                for z in range(2):
                    z = 2 * half + z
                    slot = (z - my_z) & 3
                    spread(even[n], first + 2 * z, slot)
                    spread(odd[n], first + 2 * z + 1, slot)

            inner(n).start()

    @pl.when(my_core == 0)
    def _():
        both(here, there)

    @pl.when(my_core != 0)
    def _():
        both(there, here)

    for copy in edges:
        copy.start()
    for copy in [inner(n) for n in range(4)] + edges:
        copy.wait()


def decode(meta, here, there, columns):
    return pl.pallas_call(
        functools.partial(decode_kernel, columns=columns),
        in_specs=[pl.BlockSpec(memory_space=pltpu.SMEM)] + [pl.BlockSpec(memory_space=pltpu.VMEM)] * 8,
        out_specs=pl.BlockSpec(memory_space=pl.ANY),
        out_shape=jax.ShapeDtypeStruct((1, columns, 9, VEC, VEC), jnp.float32),
        scratch_shapes=[pltpu.VMEM((columns, 9, VEC, VEC), jnp.float32), pltpu.SemaphoreType.DMA((9,))],
        compiler_params=pltpu.CompilerParams(vmem_limit_bytes=20 * MIB),
        cost_estimate=pl.CostEstimate(flops=10000000, bytes_accessed=12000000, transcendentals=0),
        name="decode",
    )(meta, *here, *there)


def stack_lines_kernel(before, middle, after, lines, left, right):
    width = MARGIN + 1
    for first, part in ((0, before), (width, middle), (width + CX, after)):
        rows = slice(first, first + part.shape[0])
        lines[rows] = part[...]
        left[rows] = part[:, :width]
        right[rows] = part[:, CX - width :]


def stack_lines(before, middle, after):
    rows, width = CX + 2 * (MARGIN + 1), MARGIN + 1
    return pl.pallas_call(
        stack_lines_kernel,
        out_shape=[jax.ShapeDtypeStruct((rows, columns, NZ), jnp.float32) for columns in (CX, width, width)],
        compiler_params=pltpu.CompilerParams(vmem_limit_bytes=4 * MIB),
        cost_estimate=pl.CostEstimate(flops=16000000000, bytes_accessed=1000000, transcendentals=0),
        name="stack_lines",
    )(before, middle, after)


def body(coarse_vectors, stiffness, vector_counts):
    rows, columns = lax.axis_size("sx"), lax.axis_size("sy")
    row, col = lax.axis_index("sx"), lax.axis_index("sy")
    mirrored = 1 - row % 2
    cv = jnp.transpose(coarse_vectors, (0, 2, 3, 1, 4))

    def halo(x, axis, dim):
        peers, length, width = lax.axis_size(axis), x.shape[dim], MARGIN + 1
        up = [(i, i + 1) for i in range(peers - 1)]
        down = [(j, i) for i, j in up]
        before = lax.ppermute(lax.slice_in_dim(x, length - width, length, axis=dim), axis, up)
        after = lax.ppermute(lax.slice_in_dim(x, 0, width, axis=dim), axis, down)
        return before, after

    before, after = halo(stiffness, "sx", 0)
    counts, before, after = lax.optimization_barrier((vector_counts, before, after))
    u, strip, down_a, down_b = pack(counts, cv)

    both = ("sx", "sy")
    number = lambda r, c: r * columns + c
    sides, diagonal, partner = [], [], []
    for r in range(rows):
        toward = 1 if r % 2 else -1
        for c in range(columns):
            if 0 <= c + toward < columns:
                sides.append((number(r, c + toward), number(r, c)))
                if c + toward == c ^ 1:
                    partner.append((number(r, c + toward), number(r, c)))
                elif r > 0:
                    diagonal.append((number(r - 1, c + toward), number(r, c)))
    high_y = lax.ppermute(strip, both, sides)
    far = lax.ppermute(down_a, both, diagonal)
    before, after, down_b = lax.optimization_barrier((before, after, down_b))
    lines, left, right = stack_lines(before, stiffness, after)
    along = [(c, c + 1) for c in range(columns - 1)]
    before = lax.ppermute(right, "sy", along)
    after = lax.ppermute(left, "sy", [(target, source) for source, target in along])
    before, after, down_a = lax.optimization_barrier((before, after, down_a))
    next_row = [(r, r + 1) for r in range(rows - 1)]
    low_a = lax.ppermute(down_a, "sx", next_row)
    low_b = lax.ppermute(down_b, "sx", next_row)

    rim = jnp.concatenate([before, lines, after], axis=1)
    rim = jnp.where(mirrored == 1, rim[:, ::-1], rim)
    rim = jnp.concatenate([rim, rim], axis=2)
    applied01, applied2a, applied2b, side01, side2, *first, far_block = own(u, high_y, far, rim)
    low_a, low_b, far_block = lax.optimization_barrier((low_a, low_b, far_block))
    partner_x = lax.ppermute(low_a, both, partner)
    second = below(applied01, applied2a, side01, side2, low_a, low_b)
    near = (col % 2 == 1 - row % 2).astype(jnp.int32)[None]
    mine, theirs = corner_and_code(near, applied01, applied2b, partner_x, (far_block, *first, *second))
    got = lax.ppermute(theirs, "sx", [(r + 1, r) for r in range(rows - 1)])
    pay = mine + jnp.pad(got, ((2 * VEC, 0), (0, 0)))

    def ring(d_y, d_z, d_core):
        out = []
        for target in range(columns):
            y, z, core = target // 8, target % 8 // 2, target % 2
            out.append(((y + d_y) % 4 * 8 + (z + d_z) % 4 * 2 + (core ^ d_core), target))
        return out

    def everyone(x, d_y, d_z):
        return [x] + [lax.ppermute(x, "sy", ring(n * d_y, n * d_z, 0)) for n in (1, 2, 3)]

    line = jnp.stack(everyone(pay, 0, 1))
    here = everyone(line, 1, 0)
    there = [lax.ppermute(part, "sy", ring(0, 0, 1)) for part in here]
    place = jnp.stack([mirrored, col // 8, col % 8 // 2, col % 2]).astype(jnp.int32)
    return decode(place, here, there, columns)


def solution(mesh):
    return jax.shard_map(
        body,
        mesh=mesh,
        in_specs=(P(None, None, "sx", "sy", None), P("sx", "sy", None), P("sx", "sy")),
        out_specs=P("sx", None, None, None, None),
        check_vma=False,
    )
```

```python
import functools

import jax
import jax.numpy as jnp
from jax import lax
from jax.experimental import pallas as pl
from jax.experimental.pallas import tpu as pltpu
from jax.sharding import PartitionSpec as P

MARGIN = 2
CX = 5
CY = 5
MASS = 0.5
EXT = 9
STRIP = 5
ABOVE = EXT - STRIP
VEC = 64
NZ = 64
L = 128
ROWS = 96
CODE_MAX = 32767.0
MIB = 1024 * 1024
VMEM = 56 * MIB

NT = (((1,), (1,)), ((), ()))


def pairs(values):
    low = lax.broadcasted_iota(jnp.int32, values[0].shape, 1) < NZ
    out = []
    for at in range(0, len(values), 2):
        first = values[at]
        if at + 1 < len(values):
            second = values[at + 1]
            top = jnp.where(low, first, pltpu.roll(second, NZ, 1))
            bottom = jnp.where(low, pltpu.roll(first, NZ, 1), second)
        else:
            top = jnp.where(low, first, 0.0)
            bottom = jnp.where(low, pltpu.roll(first, NZ, 1), 0.0)
        out.append(jnp.concatenate([top, bottom], axis=0))
    return out


def split(value):
    high = value.astype(jnp.bfloat16)
    low = (value - high.astype(jnp.float32)).astype(jnp.bfloat16)
    return high, low


def pack_kernel(counts, cv, *refs):
    outs, stages, (rows, mask, sems, out_sems) = refs[:4], refs[4:8], refs[8:]
    own, strip, below_a, below_b = stages
    row, col = lax.axis_index("sx"), lax.axis_index("sy")
    count, mirrored = counts[0, 0], 1 - lax.rem(row, 2)
    cells_x, cells_y = CX * lax.axis_size("sx"), CY * lax.axis_size("sy")

    def fetch(a):
        return pltpu.make_async_copy(cv.at[:, a], rows.at[a], sems.at[a])

    def leave(n, a):
        return pltpu.make_async_copy(stages[n].at[a], outs[n].at[a], out_sems.at[n, a])

    @pl.loop(0, EXT)
    def _(a):
        fetch(a).start()

    index01 = lax.broadcasted_iota(jnp.int32, (VEC, L), 0)
    lane = lax.broadcasted_iota(jnp.int32, (VEC // 2, L), 1)
    index2 = lax.broadcasted_iota(jnp.int32, (VEC // 2, L), 0) + jnp.where(lane < NZ, 0, VEC // 2)
    index = jnp.concatenate([index01, index2], axis=0)
    mask[0] = jnp.zeros((ROWS, L), jnp.bfloat16)
    mask[1] = (index < count).astype(jnp.float32).astype(jnp.bfloat16)

    def cells(a):
        fetch(a).wait()
        x = row * CX - MARGIN + a
        in_x = (x >= 0) & (x < cells_x)
        for b in range(EXT):
            place = jnp.where(mirrored == 1, EXT - 1 - b, b)
            y = col * CY - MARGIN + place
            keep = jnp.where(in_x & (y >= 0) & (y < cells_y), 1, 0)
            zero, one, two = (rows[a, component, place] for component in range(3))
            both = jnp.concatenate([zero, one], axis=1)
            last = jnp.concatenate([two[: VEC // 2], two[VEC // 2 :]], axis=1)
            cell = jnp.concatenate([both, last], axis=0) * mask[keep]
            own[a, :, b * L : (b + 1) * L] = cell
            if b < STRIP:
                strip[a, :, b * L : (b + 1) * L] = cell
            yield EXT - 1 - b, cell
        leave(1, a).start()
        leave(0, a).start()

    @pl.loop(0, ABOVE)
    def _(a):
        for _ in cells(a):
            pass

    @pl.loop(ABOVE, EXT)
    def _(a):
        at = a - ABOVE
        for b, cell in cells(a):
            if b < STRIP:
                below_a[at, :, b * L : (b + 1) * L] = cell
            else:
                below_b[at, :, (b - STRIP) * L : (b - STRIP + 1) * L] = cell
        for n in (2, 3):
            leave(n, at).start()

    for n, stage in enumerate(stages):
        @pl.loop(0, stage.shape[0])
        def _(a):
            leave(n, a).wait()


def pack(meta, cv):
    shapes = [
        (EXT, ROWS, EXT * L),
        (EXT, ROWS, STRIP * L),
        (STRIP, ROWS, STRIP * L),
        (STRIP, ROWS, ABOVE * L),
    ]
    anywhere = pl.BlockSpec(memory_space=pl.ANY)
    return pl.pallas_call(
        pack_kernel,
        in_specs=[pl.BlockSpec(memory_space=pltpu.SMEM), anywhere],
        out_specs=[anywhere] * 4,
        out_shape=[jax.ShapeDtypeStruct(shape, jnp.bfloat16) for shape in shapes],
        scratch_shapes=[pltpu.VMEM(shape, jnp.bfloat16) for shape in shapes]
        + [
            pltpu.VMEM((EXT, 3, EXT, VEC, NZ), jnp.bfloat16),
            pltpu.VMEM((2, ROWS, L), jnp.bfloat16),
            pltpu.SemaphoreType.DMA((EXT,)),
            pltpu.SemaphoreType.DMA((4, EXT)),
        ],
        compiler_params=pltpu.CompilerParams(vmem_limit_bytes=VMEM),
        cost_estimate=pl.CostEstimate(flops=4000000000, bytes_accessed=9000000, transcendentals=0),
        name="pack",
    )(meta, cv)


FRAME = EXT + 2


def weights_into(stiff, wx, wy, up, down):
    lane = lax.broadcasted_iota(jnp.int32, (FRAME, L), 1)
    inner = (lane % NZ) < NZ - 1
    wx[...] = jnp.zeros_like(wx)
    wy[...] = jnp.zeros_like(wy)
    for a in range(FRAME):
        here = stiff[a]
        if a > 0:
            other = stiff[a - 1]
            wx[a, :FRAME] = jnp.where((here > 0) & (other > 0), 0.5 * (here + other), 0.0)
        left, right = here[:-1], here[1:]
        wy[a, 1:FRAME] = jnp.where((left > 0) & (right > 0), 0.5 * (left + right), 0.0)
        above = jnp.where(inner, 0.5 * (here + pltpu.roll(here, L - 1, 1)), 0.0)
        up[a, :FRAME] = above
        down[a, :FRAME] = pltpu.roll(above, 1, 1)


def apply_cell(field, weights, a, b, ra, lane_low):
    wx, wy, up, down = weights
    wxa, wxb = wx[a, b : b + 1], wx[a + 1, b : b + 1]
    wya, wyb = wy[a, b : b + 1], wy[a, b + 1 : b + 2]
    upw, dnw = up[a, b : b + 1], down[a, b : b + 1]
    fx = jnp.where(lane_low, 3.0, 1.0)
    fy = jnp.where(lane_low, 1.0, 3.0)

    def at(da, db, rows):
        return field[ra + da, rows, (b + db) * L : (b + db + 1) * L]

    out = []
    for rows, (cx, cy, cz) in ((slice(0, VEC), (fx, fy, 1.0)), (slice(VEC, ROWS), (1.0, 1.0, 3.0))):
        xa, xb, ya, yb, zu, zd = wxa * cx, wxb * cx, wya * cy, wyb * cy, upw * cz, dnw * cz
        diagonal = MASS + (xa + xb) + (ya + yb) + (zu + zd)
        u = at(0, 0, rows)
        total = diagonal * u - xa * at(-1, 0, rows) - xb * at(1, 0, rows)
        total = total - ya * at(0, -1, rows) - yb * at(0, 1, rows)
        total = total - zu * pltpu.roll(u, L - 1, 1) - zd * pltpu.roll(u, 1, 1)
        out.append(total)
    return out


FIRST = FRAME - 1 - STRIP

dot = functools.partial(lax.dot_general, dimension_numbers=NT, preferred_element_type=jnp.float32)


def total(acc):
    return acc[:VEC] + acc[VEC:]


def store_split(target, a, n, value):
    high, low = split(value)
    target[a, :VEC, n * L : (n + 1) * L] = high
    target[a, VEC:, n * L : (n + 1) * L] = low


def own_kernel(
    u, high_y, far, stiff, applied01, applied2a, applied2b, side01, side2, first_tile, first_level, far_block,
    wx, wy, up, down, field, row01, row2a, row2b, acc, acc_y, acc_c,
):
    weights_into(stiff, wx, wy, up, down)
    weights = (wx, wy, up, down)
    lane_low = lax.broadcasted_iota(jnp.int32, (1, L), 1) < NZ
    field[0] = jnp.zeros((ROWS, (FRAME + 1) * L), jnp.float32)
    field[1] = jnp.zeros((ROWS, (FRAME + 1) * L), jnp.float32)
    field[FRAME] = jnp.zeros((ROWS, (FRAME + 1) * L), jnp.float32)

    @pl.loop(0, EXT)
    def _(a):
        field[a + 2, :, 0:L] = jnp.zeros((ROWS, L), jnp.float32)
        field[a + 2, :, L : (EXT + 1) * L] = u[a].astype(jnp.float32)
        field[a + 2, :, (EXT + 1) * L : (FRAME + 1) * L] = jnp.zeros((ROWS, 2 * L), jnp.float32)

    acc[...] = jnp.zeros_like(acc)
    acc_y[...] = jnp.zeros_like(acc_y)

    def applied_row(a, to01, to2a, to2b, at):
        thirds = []
        for b in range(1, FRAME):
            first, third = apply_cell(field, weights, a, b, a + 1, lane_low)
            store_split(to01, at, b - 1, first)
            thirds.append(third)
        for target, cells in ((to2a, thirds[:EXT]), (to2b, thirds[STRIP:])):
            for n, value in enumerate(pairs(cells)):
                store_split(target, at, n, value)

    def contract_row(a, from01, from2a, from2b, at):
        acc[...] += dot(from01[at, :, : EXT * L], u[a - 1, :VEC]) + dot(from2a[at], thirds_of(u, a - 1, EXT))
        acc_y[...] += dot(from01[at, :, FIRST * L :], high_y[a - 1, :VEC]) + dot(
            from2b[at], thirds_of(high_y, a - 1, STRIP)
        )

    def contract_corner(a):
        acc_c[...] += dot(applied01[a, :, FIRST * L :], far[a, :VEC]) + dot(applied2b[a], thirds_of(far, a, STRIP))

    acc_c[...] = jnp.zeros_like(acc_c)
    applied_row(0, applied01, applied2a, applied2b, 0)
    contract_corner(0)

    @pl.loop(1, STRIP)
    def _(a):
        applied_row(a, applied01, applied2a, applied2b, a)
        contract_row(a, applied01, applied2a, applied2b, a)
        contract_corner(a)

    @pl.loop(STRIP, FRAME - 1)
    def _(a):
        applied_row(a, row01, row2a, row2b, a % 2)
        contract_row(a, row01, row2a, row2b, a % 2)

    own_block, block_y = total(acc), total(acc_y)
    level = scale_of(own_block, block_y)
    first_tile[...] = code(lane_join(own_block, block_y), level)
    first_level[...] = jnp.broadcast_to(level, (8, L))
    far_block[...] = total(acc_c)

    wide = slice(4 * L, FRAME * L)
    field[0, :, wide] = jnp.zeros((ROWS, (STRIP + 2) * L), jnp.float32)
    field[1, :, wide] = jnp.zeros((ROWS, (STRIP + 2) * L), jnp.float32)
    for a in range(STRIP):
        field[a + 2, :, 4 * L : 6 * L] = jnp.zeros((ROWS, 2 * L), jnp.float32)
        field[a + 2, :, 6 * L : FRAME * L] = high_y[a].astype(jnp.float32)

    @pl.loop(0, STRIP)
    def _(a):
        thirds = []
        for n in range(STRIP):
            both, third = apply_cell(field, weights, a, n + 5, a + 1, lane_low)
            store_split(side01, a, n, both)
            thirds.append(third)
        for n, value in enumerate(pairs(thirds)):
            store_split(side2, a, n, value)


def own(u, high_y, far, stiff):
    weight = pltpu.VMEM((FRAME, 16, L), jnp.float32)
    half = lambda width, rows=STRIP: (rows, 2 * VEC, width * L)
    acc = pltpu.VMEM((2 * VEC, VEC), jnp.float32)
    return pl.pallas_call(
        own_kernel,
        out_shape=[jax.ShapeDtypeStruct(half(width), jnp.bfloat16) for width in (FRAME - 1, 5, 3, 5, 3)]
        + coded_shapes(1)
        + [jax.ShapeDtypeStruct((VEC, VEC), jnp.float32)],
        scratch_shapes=[weight] * 4
        + [pltpu.VMEM((FRAME + 1, ROWS, (FRAME + 1) * L), jnp.float32)]
        + [pltpu.VMEM(half(width, 2), jnp.bfloat16) for width in (FRAME - 1, 5, 3)]
        + [acc, acc, acc],
        compiler_params=pltpu.CompilerParams(vmem_limit_bytes=VMEM),
        cost_estimate=pl.CostEstimate(flops=14000000000, bytes_accessed=30000000, transcendentals=0),
        name="own",
    )(u, high_y, far, stiff)


def coded_shapes(tiles):
    return [jax.ShapeDtypeStruct((VEC, L), jnp.int16)] * tiles + [jax.ShapeDtypeStruct((8, L), jnp.float32)]


def lane_join(left, right):
    return jnp.concatenate([left, right], axis=1)


def scale_of(*blocks):
    largest = functools.reduce(jnp.maximum, [jnp.abs(block) for block in blocks])
    largest = jnp.max(jnp.max(largest, axis=0, keepdims=True), axis=1, keepdims=True)
    return jnp.clip(jnp.ceil(jnp.log2(largest)), -100.0, 120.0)


def code(tile, exponent):
    size = jnp.minimum(jnp.sqrt(jnp.abs(tile) * jnp.exp2(-exponent)) * CODE_MAX, CODE_MAX) + 0.5
    size = size.astype(jnp.int32)
    return jnp.where(tile < 0, -size, size).astype(jnp.int16)


def thirds_of(ref, a, cells):
    third = ref[a, VEC:].astype(jnp.float32)
    third = pairs([third[:, b * L : (b + 1) * L] for b in range(cells)])
    return jnp.concatenate(third, axis=1).astype(jnp.bfloat16)


def bring(sources, slots, sems, begin=(0,) * 6):
    def copy(n, a):
        source = sources[n].at[a, :, pl.ds(begin[n], slots[n].shape[2])]
        return pltpu.make_async_copy(source, slots[n].at[a], sems.at[n, a])

    def start(which=None):
        for a in range(STRIP):
            for n in range(len(sources)):
                if which is None or n in which:
                    copy(n, a).start()

    def wait(a, which=None):
        for n in range(len(sources)):
            if which is None or n in which:
                copy(n, a).wait()

    return start, wait


def row_shapes(widths):
    return [pltpu.VMEM((STRIP, rows, width * L), jnp.bfloat16) for rows, width in widths]


BELOW = ((2 * VEC, FRAME - 1), (2 * VEC, 5), (2 * VEC, 5), (2 * VEC, 3), (ROWS, STRIP), (ROWS, ABOVE))


def below_kernel(*refs):
    sources, (tile, turned, level), slots, (sems,) = refs[:6], refs[6:9], refs[9:15], refs[15:]
    start, wait = bring(sources, slots, sems)
    start()
    applied01, applied2a, side01, side2, low_a, low_b = slots
    sum_x, sum_d = [], []
    for a in range(STRIP):
        wait(a)
        thirds = [low_a[a, VEC:, b * L : (b + 1) * L].astype(jnp.float32) for b in range(STRIP)]
        thirds += [low_b[a, VEC:, b * L : (b + 1) * L].astype(jnp.float32) for b in range(ABOVE)]
        row = jnp.concatenate(pairs(thirds), axis=1).astype(jnp.bfloat16)
        sum_x += [
            dot(applied01[a, :, : STRIP * L], low_a[a, :VEC]),
            dot(applied01[a, :, STRIP * L : EXT * L], low_b[a, :VEC]),
            dot(applied2a[a], row),
        ]
        row = jnp.concatenate(pairs(thirds[ABOVE:]), axis=1).astype(jnp.bfloat16)
        sum_d += [
            dot(side01[a, :, :L], low_a[a, :VEC, ABOVE * L :]),
            dot(side01[a, :, L:], low_b[a, :VEC]),
            dot(side2[a], row),
        ]
    block_x, block_d = total(sum(sum_x)), total(sum(sum_d))
    exponent = scale_of(block_x, block_d)
    tile[...] = code(lane_join(block_x, block_d), exponent)
    turned[...] = code(lane_join(block_x.T, block_d.T), exponent)
    level[...] = jnp.broadcast_to(exponent, (8, L))


def below(applied01, applied2a, side01, side2, low_a, low_b):
    return pl.pallas_call(
        below_kernel,
        in_specs=[pl.BlockSpec(memory_space=pl.ANY)] * 6,
        out_shape=coded_shapes(2),
        scratch_shapes=row_shapes(BELOW) + [pltpu.SemaphoreType.DMA((6, STRIP))],
        compiler_params=pltpu.CompilerParams(vmem_limit_bytes=VMEM),
        cost_estimate=pl.CostEstimate(flops=2000000000, bytes_accessed=6000000, transcendentals=0),
        name="below",
    )(applied01, applied2a, side01, side2, low_a, low_b)


CORNER = ((2 * VEC, STRIP), (2 * VEC, 3), (ROWS, STRIP))


def corner_kernel(meta, *refs):
    sources, coded, (mine, theirs), slots, (sems, block) = refs[:3], refs[3:9], refs[9:11], refs[11:14], refs[14:]
    far_block, first_tile, first_level, second_tile, second_turned, second_level = coded
    start, wait = bring(sources, slots, sems, (FIRST * L, 0, 0))
    applied01, applied2b, partner = slots

    @pl.when(meta[0] == 1)
    def _():
        start()
        parts = []
        for a in range(STRIP):
            wait(a)
            parts.append(dot(applied01[a], partner[a, :VEC]))
            parts.append(dot(applied2b[a], thirds_of(partner, a, STRIP)))
        block[...] = total(sum(parts))

    @pl.when(meta[0] != 1)
    def _():
        block[...] = far_block[...]

    block = block[...]
    exponent = scale_of(block)
    nothing = jnp.zeros((VEC, VEC), jnp.float32)
    mine[:VEC] = first_tile[...]
    mine[VEC : 2 * VEC] = second_tile[...]
    mine[2 * VEC : 3 * VEC] = jnp.zeros((VEC, L), jnp.int16)
    mine[3 * VEC : 4 * VEC] = code(lane_join(block, nothing), exponent)
    theirs[:VEC] = second_turned[...]
    theirs[VEC : 2 * VEC] = code(lane_join(nothing, block.T), exponent)
    row = lax.broadcasted_iota(jnp.int32, (16, L), 0)
    low = lax.broadcasted_iota(jnp.int32, (16, L), 1) < NZ
    first, second = first_level[0:1, 0:1].astype(jnp.int32), second_level[0:1, 0:1].astype(jnp.int32)
    third = exponent.astype(jnp.int32)
    own_levels = jnp.where(row == 0, first, jnp.where(row == 1, second, jnp.where((row == 3) & low, third, 0)))
    their_levels = jnp.where(row == 2, second, jnp.where((row == 3) & ~low, third, 0))
    mine[4 * VEC : 4 * VEC + 16] = own_levels.astype(jnp.int16)
    theirs[2 * VEC : 2 * VEC + 16] = their_levels.astype(jnp.int16)


def corner_and_code(meta, applied01, applied2b, partner_x, coded):
    vmem = pl.BlockSpec(memory_space=pltpu.VMEM)
    anywhere = pl.BlockSpec(memory_space=pl.ANY)
    return pl.pallas_call(
        corner_kernel,
        in_specs=[pl.BlockSpec(memory_space=pltpu.SMEM)] + [anywhere] * 3 + [vmem] * 6,
        out_shape=[
            jax.ShapeDtypeStruct((4 * VEC + 16, L), jnp.int16),
            jax.ShapeDtypeStruct((2 * VEC + 16, L), jnp.int16),
        ],
        scratch_shapes=row_shapes(CORNER)
        + [pltpu.SemaphoreType.DMA((3, STRIP)), pltpu.VMEM((VEC, VEC), jnp.float32)],
        compiler_params=pltpu.CompilerParams(vmem_limit_bytes=VMEM),
        cost_estimate=pl.CostEstimate(flops=1500000000, bytes_accessed=5000000, transcendentals=0),
        name="corner",
    )(meta, applied01, applied2b, partner_x, *coded)


def decode_kernel(meta, *refs, columns):
    here, there, (out, blocks, sems) = refs[:4], refs[4:8], refs[8:]
    mirrored = meta[0] == 1
    my_y, my_z, my_core = meta[1], meta[2], meta[3]
    i_y = jnp.where(mirrored, 3, 5)
    i_yt = jnp.where(mirrored, 5, 3)
    i_c = jnp.where(mirrored, 0, 2)
    i_d = jnp.where(mirrored, 2, 0)
    i_dn = jnp.where(mirrored, 8, 6)
    i_cn = jnp.where(mirrored, 6, 8)
    step = jnp.where(mirrored, -1, 1)

    def spread(ref, c, slot):
        to_own = (c + step + columns) & (columns - 1)
        to_next = (c - step + columns) & (columns - 1)
        level = jnp.exp2(ref[slot, 4 * VEC : 4 * VEC + 16].astype(jnp.float32)) * (1.0 / (CODE_MAX * CODE_MAX))

        def value(part):
            code = ref[slot, part * VEC : (part + 1) * VEC].astype(jnp.float32)
            return code * jnp.abs(code) * level[part : part + 1]

        tile = value(0)
        blocks[c, 4] = tile[:, :NZ]
        other = tile[:, NZ:]
        blocks[c, i_y] = other
        blocks[to_own, i_yt] = other.T
        tile = value(1)
        blocks[c, 1] = tile[:, :NZ]
        blocks[to_own, i_d] = tile[:, NZ:]
        tile = value(2)
        blocks[c, 7] = tile[:, :NZ]
        blocks[c, i_dn] = tile[:, NZ:]
        tile = value(3)
        blocks[c, i_c] = tile[:, :NZ]
        blocks[to_next, i_cn] = tile[:, NZ:]

    def move(first, count, sem):
        return pltpu.make_async_copy(blocks.at[pl.ds(first, count)], out.at[0, pl.ds(first, count)], sems.at[sem])

    def inner(n):
        return move(((my_y + n) & 3) * 8 + 1, 6, n)

    edges = [move(0, 1, 4), move(columns - 1, 1, 5)] + [move(8 * y - 1, 2, 5 + y) for y in (1, 2, 3)]

    def both(even, odd):
        for n in range(4):
            first = ((my_y + n) & 3) * 8

            @pl.loop(0, 2)
            def _(half):
                for z in range(2):
                    z = 2 * half + z
                    slot = (z - my_z) & 3
                    spread(even[n], first + 2 * z, slot)
                    spread(odd[n], first + 2 * z + 1, slot)

            inner(n).start()

    @pl.when(my_core == 0)
    def _():
        both(here, there)

    @pl.when(my_core != 0)
    def _():
        both(there, here)

    for copy in edges:
        copy.start()
    for copy in [inner(n) for n in range(4)] + edges:
        copy.wait()


def decode(meta, here, there, columns):
    return pl.pallas_call(
        functools.partial(decode_kernel, columns=columns),
        in_specs=[pl.BlockSpec(memory_space=pltpu.SMEM)] + [pl.BlockSpec(memory_space=pltpu.VMEM)] * 8,
        out_specs=pl.BlockSpec(memory_space=pl.ANY),
        out_shape=jax.ShapeDtypeStruct((1, columns, 9, VEC, VEC), jnp.float32),
        scratch_shapes=[pltpu.VMEM((columns, 9, VEC, VEC), jnp.float32), pltpu.SemaphoreType.DMA((9,))],
        compiler_params=pltpu.CompilerParams(vmem_limit_bytes=20 * MIB),
        cost_estimate=pl.CostEstimate(flops=10000000, bytes_accessed=12000000, transcendentals=0),
        name="decode",
    )(meta, *here, *there)


def stack_lines_kernel(before, middle, after, lines, left, right):
    width = MARGIN + 1
    for first, part in ((0, before), (width, middle), (width + CX, after)):
        rows = slice(first, first + part.shape[0])
        lines[rows] = part[...]
        left[rows] = part[:, :width]
        right[rows] = part[:, CX - width :]


def stack_lines(before, middle, after):
    rows, width = CX + 2 * (MARGIN + 1), MARGIN + 1
    return pl.pallas_call(
        stack_lines_kernel,
        out_shape=[jax.ShapeDtypeStruct((rows, columns, NZ), jnp.float32) for columns in (CX, width, width)],
        compiler_params=pltpu.CompilerParams(vmem_limit_bytes=4 * MIB),
        cost_estimate=pl.CostEstimate(flops=16000000000, bytes_accessed=1000000, transcendentals=0),
        name="stack_lines",
    )(before, middle, after)


def body(coarse_vectors, stiffness, vector_counts):
    rows, columns = lax.axis_size("sx"), lax.axis_size("sy")
    row, col = lax.axis_index("sx"), lax.axis_index("sy")
    mirrored = 1 - row % 2
    cv = jnp.transpose(coarse_vectors, (0, 2, 3, 1, 4))

    def halo(x, axis, dim):
        peers, length, width = lax.axis_size(axis), x.shape[dim], MARGIN + 1
        up = [(i, i + 1) for i in range(peers - 1)]
        down = [(j, i) for i, j in up]
        before = lax.ppermute(lax.slice_in_dim(x, length - width, length, axis=dim), axis, up)
        after = lax.ppermute(lax.slice_in_dim(x, 0, width, axis=dim), axis, down)
        return before, after

    before, after = halo(stiffness, "sx", 0)
    counts, before, after = lax.optimization_barrier((vector_counts, before, after))
    u, strip, down_a, down_b = pack(counts, cv)

    both = ("sx", "sy")
    number = lambda r, c: r * columns + c
    sides, diagonal, partner = [], [], []
    for r in range(rows):
        toward = 1 if r % 2 else -1
        for c in range(columns):
            if 0 <= c + toward < columns:
                sides.append((number(r, c + toward), number(r, c)))
                if c + toward == c ^ 1:
                    partner.append((number(r, c + toward), number(r, c)))
                elif r > 0:
                    diagonal.append((number(r - 1, c + toward), number(r, c)))
    high_y = lax.ppermute(strip, both, sides)
    far = lax.ppermute(down_a, both, diagonal)
    before, after, down_b = lax.optimization_barrier((before, after, down_b))
    lines, left, right = stack_lines(before, stiffness, after)
    along = [(c, c + 1) for c in range(columns - 1)]
    before = lax.ppermute(right, "sy", along)
    after = lax.ppermute(left, "sy", [(target, source) for source, target in along])
    before, after, down_a = lax.optimization_barrier((before, after, down_a))
    next_row = [(r, r + 1) for r in range(rows - 1)]
    low_a = lax.ppermute(down_a, "sx", next_row)
    low_b = lax.ppermute(down_b, "sx", next_row)

    rim = jnp.concatenate([before, lines, after], axis=1)
    rim = jnp.where(mirrored == 1, rim[:, ::-1], rim)
    rim = jnp.concatenate([rim, rim], axis=2)
    applied01, applied2a, applied2b, side01, side2, *first, far_block = own(u, high_y, far, rim)
    low_a, low_b, far_block = lax.optimization_barrier((low_a, low_b, far_block))
    partner_x = lax.ppermute(low_a, both, partner)
    second = below(applied01, applied2a, side01, side2, low_a, low_b)
    near = (col % 2 == 1 - row % 2).astype(jnp.int32)[None]
    mine, theirs = corner_and_code(near, applied01, applied2b, partner_x, (far_block, *first, *second))
    got = lax.ppermute(theirs, "sx", [(r + 1, r) for r in range(rows - 1)])
    pay = mine + jnp.pad(got, ((2 * VEC, 0), (0, 0)))

    def ring(d_y, d_z, d_core):
        out = []
        for target in range(columns):
            y, z, core = target // 8, target % 8 // 2, target % 2
            out.append(((y + d_y) % 4 * 8 + (z + d_z) % 4 * 2 + (core ^ d_core), target))
        return out

    def everyone(x, d_y, d_z):
        return [x] + [lax.ppermute(x, "sy", ring(n * d_y, n * d_z, 0)) for n in (1, 2, 3)]

    line = jnp.stack(everyone(pay, 0, 1))
    here = everyone(line, 1, 0)
    there = [lax.ppermute(part, "sy", ring(0, 0, 1)) for part in here]
    place = jnp.stack([mirrored, col // 8, col % 8 // 2, col % 2]).astype(jnp.int32)
    return decode(place, here, there, columns)


def solution(mesh):
    return jax.shard_map(
        body,
        mesh=mesh,
        in_specs=(P(None, None, "sx", "sy", None), P("sx", "sy", None), P("sx", "sy")),
        out_specs=P("sx", None, None, None, None),
        check_vma=False,
    )
```
